128 devices in a mesh: comp: 2 (over z_hi), gy: 8 (over x, z_lo), gx: 8 (over y, core).
Axes of the slice: x: 4, y: 4, z: 4 (z_hi: 2, z_lo: 2; z = z_hi * 2 + z_lo), core: 2. Of those that a mesh axis runs over, the one named last changes fastest.
Arguments:
- column_water: float32 [2, 16, 64, 1024], P('comp', None, 'gy', 'gx'), may hold values from 0.2 to 2
- land_soil: float32 [2, 64, 1024], P('comp', 'gy', 'gx'), may hold values from 0.1 to 0.9
- level_weight: float32 [16], replicated, may hold values from 0.01 to 0.1
- excess_weight: float32 [16], replicated, may hold values from 0.3 to 3
- soil_weight: float32 [16], replicated, may hold values from 0.3 to 3
- terrain_class: int32 [640, 10240], P('gy', 'gx'), may hold values from 0 to 15
- surface_head: float32 [2, 640, 10240], P('comp', 'gy', 'gx'), may hold values from 0 to 1
- conductivity: float32 [2, 640, 10240], P('comp', 'gy', 'gx'), may hold values from 0.02 to 0.22
- active_mask: int32 [2, 640, 10240], P('comp', 'gy', 'gx'), may hold values 0 or 1
- flow_code: int32 [2, 640, 10240], P('comp', 'gy', 'gx'), may hold values from 0 to 3
Outputs:
- coupled_state: float32 [2, 64, 1024], P('comp', 'gy', 'gx')
The draws below stay inside these ranges and needn't reach their ends.
All inputs are finite; a program needn't handle non-finite values. No bound on the sum of `active_mask` on one device may be relied on, other than what follows from the above.
Results may differ from the reference program's by a relative error of at most 0.0003.
Values sent between devices are 32-bit elements; how exact they have to be, the bound alone decides.
No kernel may reach another device: no remote copies, remote signals or barrier semaphores. Data moves between devices by JAX's collectives and lax.ppermute only.
A program may use at most 64 MiB of HBM per device.

```python
import math
import jax
import jax.numpy as jnp
from jax import lax

LEV = 16
AGG = 10
NW = 16
NSUB = 8
SWEEPS = 2
NYC = 64
NXC = 1024
NYF = 640
NXF = 10240


def with_ends(values, stream_key, smallest, largest):
    dims = values.shape
    place = [jax.random.randint(jax.random.fold_in(stream_key, axis), (), 0, dims[axis]) for axis in range(len(dims))]
    values = values.at[tuple(place)].set(smallest)
    longest = dims.index(max(dims))
    place[longest] = (place[longest] + 1) % dims[longest]
    return values.at[tuple(place)].set(largest)


def levels(stream_key, extent, shards, smallest, high):
    gain, own = 1.0, jax.random.fold_in(stream_key, 6)
    for axis_at, parts in shards:
        steps = jnp.exp(jax.random.uniform(jax.random.fold_in(own, axis_at), (parts,), jnp.float32, smallest / len(shards), high / len(shards)))
        gain = gain * jnp.repeat(steps, extent[axis_at] // parts).reshape([-1 if axis == axis_at else 1 for axis in range(len(extent))])
    return gain


def setup_inputs(seed: int = 0) -> dict:
    key_list = jax.random.split(jax.random.key(seed), 11)
    return {
        "column_water": jnp.clip(jnp.exp(math.log(2.0) - 2.3025851 * jax.random.uniform(key_list[0], (2, LEV, NYC, NXC), jnp.float32) ** levels(key_list[0], (2, LEV, NYC, NXC), ((0, 2), (2, 8), (3, 8)), -0.2, 0.2)), 0.2, 2.0),
        "land_soil": jnp.clip(0.1 + 0.79999997 * jax.random.uniform(key_list[1], (2, NYC, NXC), jnp.float32) ** levels(key_list[1], (2, NYC, NXC), ((0, 2), (1, 8), (2, 8)), -0.2, 0.2), 0.1, 0.9),
        "level_weight": jnp.clip(jnp.exp(jax.random.uniform(key_list[2], (LEV,), jnp.float32, math.log(0.01), math.log(0.1))), 0.01, 0.1),
        "excess_weight": jnp.clip(jnp.exp(jax.random.uniform(key_list[3], (NW,), jnp.float32, math.log(0.3), math.log(3.0))), 0.3, 3.0),
        "soil_weight": jnp.clip(jnp.exp(jax.random.uniform(key_list[4], (NW,), jnp.float32, math.log(0.3), math.log(3.0))), 0.3, 3.0),
        "terrain_class": with_ends(jax.random.randint(key_list[5], (NYF, NXF), 0, NW), jax.random.fold_in(key_list[5], 1), 0, NW - 1).astype(jnp.int32),
        "surface_head": jnp.clip(1.0 * jax.random.uniform(key_list[6], (2, NYF, NXF), jnp.float32) ** levels(key_list[6], (2, NYF, NXF), ((0, 2), (1, 8), (2, 8)), -0.2, 0.2), 0.0, 1.0),
        "conductivity": jnp.clip(jnp.exp(math.log(0.22) - 2.3978953 * jax.random.uniform(key_list[7], (2, NYF, NXF), jnp.float32) ** levels(key_list[7], (2, NYF, NXF), ((0, 2), (1, 8), (2, 8)), -0.2, 0.2)), 0.02, 0.22),
        "active_mask": with_ends((jax.random.randint(key_list[8], (2, NYF, NXF), 0, 10) < 9).astype(jnp.int32), jax.random.fold_in(key_list[8], 1), 0, 1),
        "flow_code": with_ends(jax.random.randint(key_list[9], (2, NYF, NXF), 0, 4), jax.random.fold_in(key_list[9], 1), 0, 3).astype(jnp.int32),
    }


diffusion_rate = 0.2
infiltration_rate = 0.05
drainage_rate = 0.1
half_point = 0.1
evaporation_scale = 0.5

def neighbours(field):
    return (field[:-2, 1:-1], field[2:, 1:-1], field[1:-1, :-2], field[1:-1, 2:])

def lookup(table, classes):
    summed = jnp.zeros(classes.shape, table.dtype)
    for number in range(table.shape[0]):
        summed = summed + jnp.where(classes == number, table[number], 0.0)
    return summed

def block_mean(field):
    rows, cols = field.shape
    return field.reshape(rows // AGG, AGG, cols // AGG, AGG).mean(axis=(1, 3))

def upsample(field):
    return jnp.repeat(jnp.repeat(field, AGG, axis=0), AGG, axis=1)

def disaggregate(coarse, weights):
    return upsample(coarse) * (weights / upsample(block_mean(weights)))

def smooth(padded, field):
    beside_all = padded[:, :-2, 1:-1] + padded[:, 2:, 1:-1] + padded[:, 1:-1, :-2] + padded[:, 1:-1, 2:]
    return field + diffusion_rate * (beside_all - 4.0 * field)

def route_step(water, moisture, keff, active, codes):
    drained = drainage_rate * active * moisture * moisture
    centre_keff = keff[1:-1, 1:-1]
    centre_water = water[1:-1, 1:-1]
    centre_moist = moisture[1:-1, 1:-1]
    spread = jnp.zeros_like(centre_water)
    for keff_side, water_side in zip(neighbours(keff), neighbours(water)):
        spread = spread + jnp.sqrt(centre_keff * keff_side) * (water_side - centre_water)
    northern, southern, western, eastern = neighbours(drained)
    code_north, code_south, code_west, code_east = neighbours(codes)
    inflow = jnp.where(code_south == 0, southern, 0.0) + jnp.where(code_north == 1, northern, 0.0)
    inflow = inflow + jnp.where(code_east == 2, eastern, 0.0) + jnp.where(code_west == 3, western, 0.0)
    soaked = infiltration_rate * centre_water / (1.0 + centre_moist)
    return (centre_water + spread - soaked, centre_moist + soaked - drained[1:-1, 1:-1] + inflow)

def reference(column_water, land_soil, level_weight, excess_weight, soil_weight, terrain_class, surface_head, conductivity, active_mask, flow_code):
    water = column_water[0]
    for counter in range(SWEEPS):
        water = smooth(jnp.pad(water, ((0, 0), (1, 1), (1, 1))), water)
    precip = lax.optimization_barrier(jnp.sum(level_weight[:, None, None] * water * water, axis=0))
    moisture = land_soil[0]
    excess = precip * moisture * moisture / (moisture * moisture + half_point)
    excess_fine = disaggregate(excess, lookup(excess_weight, terrain_class))
    soil_fine = disaggregate(moisture, lookup(soil_weight, terrain_class))
    active = active_mask[1].astype(jnp.float32)
    keff = conductivity[1] * active
    codes = flow_code[1]
    ponded = active * (surface_head[1] + excess_fine)
    stored = soil_fine
    for counter in range(NSUB):
        ponded, stored = route_step(jnp.pad(ponded, 1), jnp.pad(stored, 1), jnp.pad(keff, 1), jnp.pad(active, 1), jnp.pad(codes, 1))
    land_out = block_mean(stored) / (1.0 + evaporation_scale * water[0] * water[0])
    return jnp.stack([land_out, block_mean(ponded)])
```

```python
import jax
import jax.numpy as jnp
import numpy as np
from jax import lax
from jax.experimental import pallas as pl
from jax.experimental.pallas import tpu as pltpu
from jax.sharding import PartitionSpec as P

AGG = 10
NSUB = 8
LEV = 16
ROWS = 80
COLS = 1280
HALO = 8
STRIPS = 12
TILES = 11
WIDE = TILES * 128
FIELDS = 5
BF = jnp.bfloat16
F32 = jnp.float32

diffusion_rate = 0.2
infiltration_rate = 0.05
drainage_rate = 0.1
half_point = 0.1
evaporation_scale = 0.5


def tables():
    lane = np.arange(WIDE)
    col = np.where(lane < COLS, lane // AGG, np.where(lane < COLS + 8, 128, np.where(lane >= WIDE - 8, 255, -1)))
    up_cols = (np.arange(256)[:, None] == col[None]).astype(np.float32)
    pool_cols = up_cols[:128].T.copy()
    k, s = np.meshgrid(np.arange(STRIPS), np.arange(8), indexing="ij")
    fine = (12 * s + k).reshape(-1)
    row = np.where(fine < ROWS, fine // AGG, np.where(fine < ROWS + 8, 8, 15))
    up_rows = (row[:, None] == np.arange(16)[None]).astype(np.float32)
    pool_rows = up_rows[:, :8].T * (fine < ROWS)[None]
    own_rows = (np.arange(ROWS)[:, None] // AGG == np.arange(8)[None]).astype(np.float32)
    return dict(
        up_cols=jnp.asarray(up_cols, BF),
        pool_cols=jnp.asarray(pool_cols, BF),
        up_rows=jnp.asarray(np.concatenate([up_rows, up_rows], 1), BF),
        pool_rows=jnp.asarray(np.concatenate([pool_rows, pool_rows], 1), BF),
        own_up=jnp.asarray(np.concatenate([own_rows, own_rows], 1), BF),
        own_pool=jnp.asarray(np.concatenate([own_rows.T, own_rows.T], 1), BF),
    )


def split(x):
    high = x.astype(BF)
    return high, (x - high.astype(F32)).astype(BF)


def dot(a, b):
    return jnp.dot(a, b, preferred_element_type=F32)


def lanes():
    return lax.broadcasted_iota(jnp.int32, (8, 128), 1)


def beside(tiles, lane):
    right = [pltpu.roll(x, 1, 1) for x in tiles]
    left = [pltpu.roll(x, 127, 1) for x in tiles]
    n = len(tiles)
    west = [jnp.where(lane == 0, right[t - 1], right[t]) for t in range(n)]
    east = [jnp.where(lane == 127, left[(t + 1) % n], left[t]) for t in range(n)]
    return west, east


def cut(t):
    return slice(t * 128, (t + 1) * 128)


def pack_kernel(
    water, soil, etab, stab, terrain, head, cond, mask, code, pool_cols, up_cols, own_up, own_pool,
    gxl, gxr, main_up, main_down, gyu, gyd, keff_out, ew_out, sw_out, square,
):
    group = lax.axis_index("comp")

    @pl.when(group == 0)
    def _():
        square[...] = water[...].T
        gxl[0:8] = square[0:8]
        gxr[0:8] = square[120:128]
        square[0:8] = soil[...]
        square[8:128] = jnp.zeros((120, 128), F32)
        turned = square[...].T
        gxl[8:16] = turned[0:8]
        gxr[8:16] = turned[120:128]
        gxl[16:40] = jnp.zeros((24, 128), F32)
        gxr[16:40] = jnp.zeros((24, 128), F32)
        for j in range(3):
            for h in range(2):
                at = j * 16 + h * 8
                main_up[at : at + 8] = water[pl.ds(h * 64 + j, 8, stride=8), :]
                main_down[at : at + 8] = water[pl.ds(h * 64 + 5 + j, 8, stride=8), :]
        main_up[48:56] = soil[...]
        main_down[48:56] = soil[...]

    @pl.when(group == 1)
    def _():
        ebig = jnp.broadcast_to(etab[...], (8, 128))
        sbig = jnp.broadcast_to(stab[...], (8, 128))
        for r in range(0, ROWS, 8):
            for t in range(10):
                at = terrain[r : r + 8, cut(t)]
                ew_out[r : r + 8, cut(t)] = jnp.take_along_axis(ebig, at, axis=1)
                sw_out[r : r + 8, cut(t)] = jnp.take_along_axis(sbig, at, axis=1)
        for out in (ew_out, sw_out):
            high, low = split(out[...])
            part = dot(high, pool_cols[0:COLS]) + dot(low, pool_cols[0:COLS])
            high, low = split(part)
            total = dot(own_pool[...], jnp.concatenate([high, low], axis=0))
            high, low = split(float(AGG * AGG) / total)
            wide = dot(jnp.concatenate([high, low], axis=0), up_cols[0:128, 0:COLS]).astype(BF)
            out[...] = out[...] * dot(own_up[...], wide)
        keff_out[...] = cond[...] * mask[...].astype(F32)
        fields = (
            lambda r, c: keff_out[r, c],
            lambda r, c: head[r, c],
            lambda r, c: code[r, c].astype(F32),
            lambda r, c: ew_out[r, c],
            lambda r, c: sw_out[r, c],
        )
        for f, field in enumerate(fields):
            for t in range(10):
                at = f * 80 + t * 8
                gyu[at : at + 8] = field(slice(0, 8), cut(t))
                gyd[at : at + 8] = field(slice(ROWS - 8, ROWS), cut(t))
        lane = lax.broadcasted_iota(jnp.int32, (ROWS, 128), 1)
        edges = jnp.zeros((ROWS, 128), F32)
        for f, field in enumerate(fields):
            first = field(slice(0, ROWS), cut(0))
            last = field(slice(0, ROWS), cut(9))
            first = first if f == 0 else pltpu.roll(first, 8 * f, 1)
            last = pltpu.roll(last, (64 + 8 * f - 120) % 128, 1)
            edges = jnp.where(lane // 8 == f, first, edges)
            edges = jnp.where(lane // 8 == 8 + f, last, edges)
        square[0:ROWS] = edges
        square[ROWS:128] = jnp.zeros((128 - ROWS, 128), F32)
        square[...] = square[...].T
        gxl[...] = square[0:40]
        gxr[...] = square[64:104]


def middle_kernel(
    water, soil, weight, keff, head, code, ew, sw, from_left, from_right, from_up, from_down, rows_up, rows_down,
    coarse, water_out, a_e, a_w, a_n, a_s, a_c, m_e, m_w, m_n, m_s, m_c, head_out, ew_out, sw_out,
    square, side, nat, kring, cring,
):
    group = lax.axis_index("comp")
    gy, gx = lax.axis_index("gy"), lax.axis_index("gx")
    has_up = (gy > 0).astype(F32)
    has_down = (gy < lax.axis_size("gy") - 1).astype(F32)
    has_left = (gx > 0).astype(F32)
    has_right = (gx < lax.axis_size("gx") - 1).astype(F32)

    @pl.when(group == 0)
    def _():
        pairs = (
            (from_right[0:8], from_left[0:8]),
            (from_down[16:24], from_down[0:8]),
            (from_up[16:24], from_up[0:8]),
        )
        square[8:120] = jnp.zeros((112, 128), F32)
        for i, (right, left) in enumerate(pairs):
            square[0:8] = right
            square[120:128] = left
            side[i] = square[...].T
        lane = lanes()
        for at, (own, down, up) in (
            (0, (from_right[8:16], from_down[24:32], from_up[24:32])),
            (120, (from_left[8:16], from_down[8:16], from_up[8:16])),
        ):
            square[at : at + 8] = jnp.where(
                lane < 8, own, jnp.where(lane < 16, pltpu.roll(down, 8, 1), pltpu.roll(up, 16, 1))
            )
        side_soil = square[...].T

        lane2 = lax.broadcasted_iota(jnp.int32, (1, 256), 1)
        col_ok = jnp.where(lane2 < 128, 1.0, jnp.where(lane2 < 192, has_right, has_left))

        def levels(ref, row):
            return jnp.concatenate(
                [ref[pl.ds(h * 64 + row, 8, stride=8), :] for h in range(2)], axis=0
            )

        def side_levels(i, row):
            return jnp.concatenate(
                [side[i, pl.ds(h * 64 + row, 8, stride=8), :] for h in range(2)], axis=0
            )

        field = []
        for j in range(3):
            tile = from_up[32 + j * 16 : 48 + j * 16]
            field.append(jnp.concatenate([tile, side_levels(2, 5 + j)], axis=1) * (col_ok * has_up))
        for j in range(8):
            field.append(jnp.concatenate([levels(water, j), side_levels(0, j)], axis=1) * col_ok)
        for j in range(3):
            tile = from_down[32 + j * 16 : 48 + j * 16]
            field.append(jnp.concatenate([tile, side_levels(1, j)], axis=1) * (col_ok * has_down))

        def sweep(old, first, last):
            new = {}
            for q in range(first, last):
                around = old[q - 1] + old[q + 1] + pltpu.roll(old[q], 1, 1) + pltpu.roll(old[q], 255, 1)
                new[q] = old[q] + diffusion_rate * (around - 4.0 * old[q])
            return new

        once = sweep(field, 1, 13)
        for q in once:
            once[q] = once[q] * (col_ok * (has_up if q < 3 else has_down if q > 10 else 1.0))
        twice = sweep(once, 2, 12)
        for j in range(8):
            water_out[j : j + 1] = twice[3 + j][0:1, 0:128]
        level_weight = jnp.broadcast_to(weight[...], (LEV, 256))
        rain = {q: jnp.sum(level_weight * twice[q] * twice[q], axis=0, keepdims=True) for q in twice}
        blank = jnp.zeros((6, 256), F32)
        rain = jnp.concatenate([rain[3 + j] for j in range(8)] + [rain[11], blank, rain[2]], axis=0)
        moist = jnp.concatenate(
            [
                jnp.concatenate([soil[...], side_soil[0:8]], axis=1),
                jnp.concatenate([from_down[80:81], side_soil[8:9]], axis=1),
                blank,
                jnp.concatenate([from_up[87:88], side_soil[23:24]], axis=1),
            ],
            axis=0,
        )
        coarse[0] = rain * moist * moist / (moist * moist + half_point)
        coarse[1] = moist

    @pl.when(group == 1)
    def _():
        lane128 = lax.broadcasted_iota(jnp.int32, (40, 128), 1)

        def column(own, down, up):
            down, up = pltpu.roll(down, 80, 1), pltpu.roll(up, 16, 1)
            return jnp.where(lane128 < 80, own, jnp.where(lane128 < 88, down * has_down, up * has_up))

        square[...] = jnp.zeros((128, 128), F32)
        square[0:40] = column(from_right[...], from_down[40:80], from_up[40:80]) * has_right
        square[64:104] = column(from_left[...], from_down[0:40], from_up[0:40]) * has_left
        side[0] = square[...].T
        own = (
            lambda c: keff[:, c],
            lambda c: head[:, c],
            lambda c: code[:, c].astype(F32),
            lambda c: ew[:, c],
            lambda c: sw[:, c],
        )
        lane = lax.broadcasted_iota(jnp.int32, (96, 128), 1)
        for f in range(FIELDS):
            for t in range(10):
                at = f * 80 + t * 8
                nat[t, 0:ROWS] = own[f](cut(t))
                nat[t, ROWS : ROWS + 8] = rows_down[at : at + 8] * has_down
                nat[t, ROWS + 8 : ROWS + 16] = rows_up[at : at + 8] * has_up
            columns = side[0, 0:96]
            right = columns if f == 0 else pltpu.roll(columns, (-8 * f) % 128, 1)
            left = pltpu.roll(columns, 120 - 64 - 8 * f, 1)
            nat[10] = jnp.where(lane < 8, right, jnp.where(lane >= 120, left, 0.0))
            for k in range(STRIPS):
                for t in range(TILES):
                    value = nat[t, pl.ds(k, 8, stride=STRIPS), :]
                    if f == 0:
                        kring[k + 1, :, cut(t)] = value
                    elif f == 1:
                        active = kring[k + 1, :, cut(t)] > 0.0
                        head_out[k, :, cut(t)] = jnp.where(active, value, 0.0)
                    elif f == 2:
                        cring[k + 1, :, cut(t)] = value
                    elif f == 3:
                        active = kring[k + 1, :, cut(t)] > 0.0
                        ew_out[k, :, cut(t)] = jnp.where(active, value, 0.0)
                    else:
                        sw_out[k, :, cut(t)] = value
        for ring in (kring, cring):
            for t in range(TILES):
                ring[0, :, cut(t)] = pltpu.roll(ring[STRIPS, :, cut(t)], 1, 0)
                ring[STRIPS + 1, :, cut(t)] = pltpu.roll(ring[1, :, cut(t)], 7, 0)

        def strip(k, carry):
            lane = lanes()
            here = [kring[k + 1, :, cut(t)] for t in range(TILES)]
            codes = [cring[k + 1, :, cut(t)] for t in range(TILES)]
            west, east = beside(here, lane)

            def drains(cond, codes, number):
                return jnp.where((cond > 0.0) & (codes == number), drainage_rate, 0.0)

            to_east, _ = beside([drains(here[t], codes[t], 3.0) for t in range(TILES)], lane)
            _, to_west = beside([drains(here[t], codes[t], 2.0) for t in range(TILES)], lane)
            for t in range(TILES):
                north, south = kring[k, :, cut(t)], kring[k + 2, :, cut(t)]
                n, s = jnp.sqrt(here[t] * north), jnp.sqrt(here[t] * south)
                w, e = jnp.sqrt(here[t] * west[t]), jnp.sqrt(here[t] * east[t])
                a_n[k, :, cut(t)] = n
                a_s[k, :, cut(t)] = s
                a_w[k, :, cut(t)] = w
                a_e[k, :, cut(t)] = e
                a_c[k, :, cut(t)] = 1.0 - ((n + s) + (w + e))
                m_n[k, :, cut(t)] = drains(north, cring[k, :, cut(t)], 1.0)
                m_s[k, :, cut(t)] = drains(south, cring[k + 2, :, cut(t)], 0.0)
                m_w[k, :, cut(t)] = to_east[t]
                m_e[k, :, cut(t)] = to_west[t]
                m_c[k, :, cut(t)] = jnp.where(here[t] > 0.0, drainage_rate, 0.0)
            return carry

        lax.fori_loop(0, STRIPS, strip, 0)


def route_kernel(
    coarse, a_e, a_w, a_n, a_s, a_c, m_e, m_w, m_n, m_s, m_c, head, ew, sw, up_cols, up_rows, pool_cols, pool_rows,
    ponded_out, stored_out, pond_a, pond_b, store_a, store_b,
):
    group = lax.axis_index("comp")

    @pl.when(group == 1)
    def _():
        pieces = jnp.concatenate([*split(coarse[0]), *split(coarse[1])], axis=0)
        wide = dot(pieces, up_cols[...]).astype(BF)
        excess = dot(up_rows[...], wide[0:32])
        moist = dot(up_rows[...], wide[32:64])
        pond_a[1 : STRIPS + 1] = head[...] + ew[...] * excess.reshape(STRIPS, 8, WIDE)
        store_a[1 : STRIPS + 1] = sw[...] * moist.reshape(STRIPS, 8, WIDE)

        def close(ring):
            for t in range(TILES):
                ring[0, :, cut(t)] = pltpu.roll(ring[STRIPS, :, cut(t)], 1, 0)
                ring[STRIPS + 1, :, cut(t)] = pltpu.roll(ring[1, :, cut(t)], 7, 0)

        close(pond_a)
        close(store_a)

        def substep(pond, store, new_pond, new_store):
            def strip(k, carry):
                lane = lanes()
                p = [pond[k + 1, :, cut(t)] for t in range(TILES)]
                s = [store[k + 1, :, cut(t)] for t in range(TILES)]
                q = [x * x for x in s]
                p_w, p_e = beside(p, lane)
                q_w, q_e = beside(q, lane)
                for t in range(TILES):
                    c = cut(t)
                    s_n, s_s = store[k, :, c], store[k + 2, :, c]
                    below = 1.0 + s[t]
                    guess = pl.reciprocal(below, approx=True)
                    guess = guess * (2.0 - below * guess)
                    soaked = infiltration_rate * p[t] * guess
                    flow = a_n[k, :, c] * pond[k, :, c] + a_s[k, :, c] * pond[k + 2, :, c]
                    flow = flow + (a_w[k, :, c] * p_w[t] + a_e[k, :, c] * p_e[t])
                    new_pond[k + 1, :, c] = a_c[k, :, c] * p[t] + flow - soaked
                    inflow = m_n[k, :, c] * (s_n * s_n) + m_s[k, :, c] * (s_s * s_s)
                    inflow = inflow + (m_w[k, :, c] * q_w[t] + m_e[k, :, c] * q_e[t])
                    new_store[k + 1, :, c] = s[t] + soaked - m_c[k, :, c] * q[t] + inflow
                return carry

            lax.fori_loop(0, STRIPS, strip, 0)
            close(new_pond)
            close(new_store)

        def two(i, carry):
            substep(pond_a, store_a, pond_b, store_b)
            substep(pond_b, store_b, pond_a, store_a)
            return carry

        lax.fori_loop(0, NSUB // 2, two, 0)
        for ring, out in ((pond_a, ponded_out), (store_a, stored_out)):
            high, low = split(ring[1 : STRIPS + 1].reshape(STRIPS * 8, WIDE))
            part = dot(high, pool_cols[...]) + dot(low, pool_cols[...])
            out[...] = dot(pool_rows[...], jnp.concatenate([*split(part)], axis=0)) * (1.0 / (AGG * AGG))


def moved(array, mesh_shape, target):
    groups, ys, xs = mesh_shape
    pairs = []
    for g in range(groups):
        for y in range(ys):
            for x in range(xs):
                a, b, c = target(g, y, x)
                pairs.append(((g * ys + y) * xs + x, ((a % groups) * ys + b % ys) * xs + c % xs))
    return lax.ppermute(array, ("comp", "gy", "gx"), pairs)


def f32(*shape):
    return jax.ShapeDtypeStruct(shape, F32)


def per_device(
    column_water,
    land_soil,
    level_weight,
    excess_weight,
    soil_weight,
    terrain_class,
    surface_head,
    conductivity,
    active_mask,
    flow_code,
):
    shape = tuple(lax.axis_size(axis) for axis in ("comp", "gy", "gx"))
    group = lax.axis_index("comp")
    m = tables()
    water = column_water[0].reshape(128, 128)
    soil = land_soil[0]
    etab = jnp.pad(excess_weight, (0, 112))[None]
    stab = jnp.pad(soil_weight, (0, 112))[None]
    params = pltpu.CompilerParams(vmem_limit_bytes=32 * 1024 * 1024)
    gxl, gxr, main_up, main_down, gyu, gyd, keff, ew, sw = pl.pallas_call(
        pack_kernel,
        out_shape=[f32(40, 128)] * 2 + [f32(56, 128)] * 2 + [f32(400, 128)] * 2 + [f32(ROWS, COLS)] * 3,
        scratch_shapes=[pltpu.VMEM((128, 128), F32)],
        compiler_params=params,
        name="pack",
    )(
        water, soil, etab, stab, terrain_class, surface_head[0], conductivity[0], active_mask[0], flow_code[0],
        m["pool_cols"], m["up_cols"], m["own_up"], m["own_pool"],
    )
    from_left = moved(gxr, shape, lambda g, y, x: (g, y, x + 1))
    from_right = moved(gxl, shape, lambda g, y, x: (g, y, x - 1))
    rows_up = moved(gyd, shape, lambda g, y, x: (g, y + g, x))
    rows_down = moved(gyu, shape, lambda g, y, x: (g, y - g, x))
    land = jnp.concatenate([from_left[:16], from_right[:16]])
    route = jnp.concatenate([from_left, from_right, jnp.zeros((8, 128), F32)])
    send_up = jnp.where(group == 0, jnp.concatenate([land, main_up]), route)
    send_down = jnp.where(group == 0, jnp.concatenate([land, main_down]), route)
    from_up = moved(send_down, shape, lambda g, y, x: (g, y + 1, x))
    from_down = moved(send_up, shape, lambda g, y, x: (g, y - 1, x))
    strips = f32(STRIPS, 8, WIDE)
    coarse, water_top, *prepared = pl.pallas_call(
        middle_kernel,
        out_shape=[f32(2, 16, 256), f32(8, 128)] + [strips] * 13,
        scratch_shapes=[
            pltpu.VMEM((128, 128), F32),
            pltpu.VMEM((3, 128, 128), F32),
            pltpu.VMEM((TILES, 96, 128), F32),
            pltpu.VMEM((STRIPS + 2, 8, WIDE), F32),
            pltpu.VMEM((STRIPS + 2, 8, WIDE), F32),
        ],
        compiler_params=params,
        name="middle",
    )(
        water, soil, level_weight[:, None], keff, surface_head[0], flow_code[0], ew, sw,
        from_left, from_right, from_up, from_down, rows_up, rows_down,
    )
    arrived = moved(coarse, shape, lambda g, y, x: (1 - g, y, x))
    ring = pltpu.VMEM((STRIPS + 2, 8, WIDE), F32)
    ponded, stored = pl.pallas_call(
        route_kernel,
        out_shape=[f32(8, 128), f32(8, 128)],
        scratch_shapes=[ring] * 4,
        compiler_params=params,
        name="route",
    )(arrived, *prepared, m["up_cols"], m["up_rows"], m["pool_cols"], m["pool_rows"])
    returned = moved(stored, shape, lambda g, y, x: (1 - g, y, x))
    land_out = returned / (1.0 + evaporation_scale * water_top * water_top)
    return jnp.where(group == 0, land_out, ponded)[None]


def solution(mesh):
    in_specs = (
        P("comp", None, "gy", "gx"),
        P("comp", "gy", "gx"),
        P(),
        P(),
        P(),
        P("gy", "gx"),
        P("comp", "gy", "gx"),
        P("comp", "gy", "gx"),
        P("comp", "gy", "gx"),
        P("comp", "gy", "gx"),
    )
    out_specs = P("comp", "gy", "gx")
    return jax.shard_map(
        per_device, mesh=mesh, in_specs=in_specs, out_specs=out_specs, check_vma=False
    )
```

```python
import jax
import jax.numpy as jnp
import numpy as np
from jax import lax
from jax.experimental import pallas as pl
from jax.experimental.pallas import tpu as pltpu
from jax.sharding import PartitionSpec as P

AGG = 10
NSUB = 8
LEV = 16
ROWS = 80
COLS = 1280
HALO = 8
STRIPS = 12
TILES = 11
WIDE = TILES * 128
CHUNKS = 1
NW = 16
FIELDS = 5
BF = jnp.bfloat16
F32 = jnp.float32

diffusion_rate = 0.2
infiltration_rate = 0.05
drainage_rate = 0.1
half_point = 0.1
evaporation_scale = 0.5


def tables():
    lane = np.arange(WIDE)
    col = np.where(lane < COLS, lane // AGG, np.where(lane < COLS + 8, 128, np.where(lane >= WIDE - 8, 255, -1)))
    up_cols = (np.arange(256)[:, None] == col[None]).astype(np.float32)
    pool_cols = up_cols[:128].T.copy()
    k, s = np.meshgrid(np.arange(STRIPS), np.arange(8), indexing="ij")
    fine = (12 * s + k).reshape(-1)
    row = np.where(fine < ROWS, fine // AGG, np.where(fine < ROWS + 8, 8, 15))
    up_rows = (row[:, None] == np.arange(16)[None]).astype(np.float32)
    pool_rows = up_rows[:, :8].T * (fine < ROWS)[None]
    return dict(
        up_cols=jnp.asarray(up_cols, BF),
        pool_cols=jnp.asarray(pool_cols, BF),
        up_rows=jnp.asarray(np.concatenate([up_rows, up_rows], 1), BF),
        pool_rows=jnp.asarray(np.concatenate([pool_rows, pool_rows], 1), BF),
    )


def split(x):
    high = x.astype(BF)
    return high, (x - high.astype(F32)).astype(BF)


def dot(a, b):
    return jnp.dot(a, b, preferred_element_type=F32)


def lanes():
    return lax.broadcasted_iota(jnp.int32, (8, 128), 1)


def beside(tiles, lane):
    right = [pltpu.roll(x, 1, 1) for x in tiles]
    left = [pltpu.roll(x, 127, 1) for x in tiles]
    n = len(tiles)
    west = [jnp.where(lane == 0, right[t - 1], right[t]) for t in range(n)]
    east = [jnp.where(lane == 127, left[(t + 1) % n], left[t]) for t in range(n)]
    return west, east


def cut(t):
    return slice(t * 128, (t + 1) * 128)


def within(shape, fine_axis):
    fine = lax.broadcasted_iota(jnp.int32, shape, fine_axis)
    first = AGG * lax.broadcasted_iota(jnp.int32, shape, 1 - fine_axis)
    return jnp.where((fine >= first) & (fine < first + AGG), 1.0, 0.0).astype(BF)


def pack_kernel(
    water_in, soil_in, weight_in, etab_in, stab_in, terrain_in, head_in, cond_in, mask_in, code_in,
    gxl, gxr, main_up, main_down, gyu, gyd, water, soil, weight, keff, head, code, ew, sw,
    square, tabs, terrain, mask, code_int, sems,
):
    group = lax.axis_index("comp")

    @pl.when(group == 0)
    def _():
        loads = [
            pltpu.make_async_copy(water_in, water, sems.at[0]),
            pltpu.make_async_copy(soil_in, soil, sems.at[1]),
            pltpu.make_async_copy(weight_in, tabs.at[0], sems.at[2]),
        ]
        for load in loads:
            load.start()
        gxl[16:40] = jnp.zeros((24, 128), F32)
        gxr[16:40] = jnp.zeros((24, 128), F32)
        square[16:128] = jnp.zeros((112, 128), F32)
        for load in loads:
            load.wait()
        square[0:8] = soil[...]
        square[8:9, 0:LEV] = tabs[0]
        turned = square[...].T
        gxl[8:16] = turned[0:8]
        gxr[8:16] = turned[120:128]
        weight[...] = jnp.broadcast_to(turned[0:LEV, 8:9], (LEV, 128))
        square[...] = water[...].T
        gxl[0:8] = square[0:8]
        gxr[0:8] = square[120:128]
        for j in range(3):
            for h in range(2):
                at = j * 16 + h * 8
                main_up[at : at + 8] = water[pl.ds(h * 64 + j, 8, stride=8), :]
                main_down[at : at + 8] = water[pl.ds(h * 64 + 5 + j, 8, stride=8), :]
        main_up[48:56] = soil[...]
        main_down[48:56] = soil[...]

    @pl.when(group == 1)
    def _():
        load_tabs = [
            pltpu.make_async_copy(etab_in, tabs.at[1], sems.at[0]),
            pltpu.make_async_copy(stab_in, tabs.at[2], sems.at[1]),
        ]
        for load in load_tabs:
            load.start()
        loads = []
        for i, (source, target) in enumerate(
            ((terrain_in, terrain), (cond_in, keff), (mask_in, mask), (head_in, head), (code_in, code_int))
        ):
            parts = []
            for j in range(CHUNKS):
                rows = pl.ds(j * (ROWS // CHUNKS), ROWS // CHUNKS)
                parts.append(pltpu.make_async_copy(source.at[rows], target.at[rows], sems.at[2 + i * CHUNKS + j]))
                parts[-1].start()
            loads.append(parts)

        def ready(i):
            for part in loads[i]:
                part.wait()

        pool_cols = within((COLS, 128), 0)
        up_cols = within((128, COLS), 1)
        up_rows, pool_rows = within((ROWS, 8), 0), within((8, ROWS), 1)
        for load in load_tabs:
            load.wait()
        ready(0)
        for i, out in ((1, ew), (2, sw)):
            big = jnp.concatenate([jnp.broadcast_to(tabs[i], (8, NW))] * (128 // NW), axis=1)
            for r in range(0, ROWS, 8):
                for t in range(10):
                    out[r : r + 8, cut(t)] = jnp.take_along_axis(big, terrain[r : r + 8, cut(t)], axis=1)
        for out in (ew, sw):
            high, low = split(out[...])
            part = dot(high, pool_cols) + dot(low, pool_cols)
            high, low = split(part)
            total = dot(pool_rows, high) + dot(pool_rows, low)
            high, low = split(float(AGG * AGG) / total)
            wide_high, wide_low = dot(high, up_cols).astype(BF), dot(low, up_cols).astype(BF)
            out[...] = out[...] * (dot(up_rows, wide_high) + dot(up_rows, wide_low))
        ready(1)
        ready(2)
        keff[...] = keff[...] * mask[...].astype(F32)
        ready(3)
        ready(4)
        code[...] = code_int[...].astype(F32)
        fields = (keff, head, code, ew, sw)
        for f, field in enumerate(fields):
            for t in range(10):
                at = f * 80 + t * 8
                gyu[at : at + 8] = field[0:8, cut(t)]
                gyd[at : at + 8] = field[ROWS - 8 : ROWS, cut(t)]
        lane = lax.broadcasted_iota(jnp.int32, (ROWS, 128), 1)
        edges = jnp.zeros((ROWS, 128), F32)
        for f, field in enumerate(fields):
            first = field[:, cut(0)]
            last = field[:, cut(9)]
            first = first if f == 0 else pltpu.roll(first, 8 * f, 1)
            last = pltpu.roll(last, (64 + 8 * f - 120) % 128, 1)
            edges = jnp.where(lane // 8 == f, first, edges)
            edges = jnp.where(lane // 8 == 8 + f, last, edges)
        square[0:ROWS] = edges
        square[ROWS:128] = jnp.zeros((128 - ROWS, 128), F32)
        square[...] = square[...].T
        gxl[...] = square[0:40]
        gxr[...] = square[64:104]


def edges_of_grid():
    gy, gx = lax.axis_index("gy"), lax.axis_index("gx")
    has_up = (gy > 0).astype(F32)
    has_down = (gy < lax.axis_size("gy") - 1).astype(F32)
    has_left = (gx > 0).astype(F32)
    has_right = (gx < lax.axis_size("gx") - 1).astype(F32)
    return has_up, has_down, has_left, has_right


def land_kernel(
    water, soil, weight, from_left, from_right, from_up, from_down, coarse, water_out, square, side,
):
    group = lax.axis_index("comp")
    has_up, has_down, has_left, has_right = edges_of_grid()

    @pl.when(group == 0)
    def _():
        pairs = (
            (from_right[0:8], from_left[0:8]),
            (from_down[16:24], from_down[0:8]),
            (from_up[16:24], from_up[0:8]),
        )
        square[8:120] = jnp.zeros((112, 128), F32)
        for i, (right, left) in enumerate(pairs):
            square[0:8] = right
            square[120:128] = left
            side[i] = square[...].T
        lane = lanes()
        for at, (own, down, up) in (
            (0, (from_right[8:16], from_down[24:32], from_up[24:32])),
            (120, (from_left[8:16], from_down[8:16], from_up[8:16])),
        ):
            square[at : at + 8] = jnp.where(
                lane < 8, own, jnp.where(lane < 16, pltpu.roll(down, 8, 1), pltpu.roll(up, 16, 1))
            )
        side_soil = square[...].T

        lane2 = lax.broadcasted_iota(jnp.int32, (1, 256), 1)
        col_ok = jnp.where(lane2 < 128, 1.0, jnp.where(lane2 < 192, has_right, has_left))

        def levels(ref, row):
            return jnp.concatenate(
                [ref[pl.ds(h * 64 + row, 8, stride=8), :] for h in range(2)], axis=0
            )

        def side_levels(i, row):
            return jnp.concatenate(
                [side[i, pl.ds(h * 64 + row, 8, stride=8), :] for h in range(2)], axis=0
            )

        field = []
        for j in range(3):
            tile = from_up[32 + j * 16 : 48 + j * 16]
            field.append(jnp.concatenate([tile, side_levels(2, 5 + j)], axis=1) * (col_ok * has_up))
        for j in range(8):
            field.append(jnp.concatenate([levels(water, j), side_levels(0, j)], axis=1) * col_ok)
        for j in range(3):
            tile = from_down[32 + j * 16 : 48 + j * 16]
            field.append(jnp.concatenate([tile, side_levels(1, j)], axis=1) * (col_ok * has_down))

        def sweep(old, first, last):
            new = {}
            for q in range(first, last):
                around = old[q - 1] + old[q + 1] + pltpu.roll(old[q], 1, 1) + pltpu.roll(old[q], 255, 1)
                new[q] = old[q] + diffusion_rate * (around - 4.0 * old[q])
            return new

        once = sweep(field, 1, 13)
        for q in once:
            once[q] = once[q] * (col_ok * (has_up if q < 3 else has_down if q > 10 else 1.0))
        twice = sweep(once, 2, 12)
        for j in range(8):
            water_out[j : j + 1] = twice[3 + j][0:1, 0:128]
        level_weight = jnp.concatenate([weight[...]] * 2, axis=1)
        rain = {q: jnp.sum(level_weight * twice[q] * twice[q], axis=0, keepdims=True) for q in twice}
        blank = jnp.zeros((6, 256), F32)
        rain = jnp.concatenate([rain[3 + j] for j in range(8)] + [rain[11], blank, rain[2]], axis=0)
        moist = jnp.concatenate(
            [
                jnp.concatenate([soil[...], side_soil[0:8]], axis=1),
                jnp.concatenate([from_down[80:81], side_soil[8:9]], axis=1),
                blank,
                jnp.concatenate([from_up[87:88], side_soil[23:24]], axis=1),
            ],
            axis=0,
        )
        coarse[0] = rain * moist * moist / (moist * moist + half_point)
        coarse[1] = moist


def prepare_kernel(
    keff, head, code, ew, sw, from_left, from_right, from_up, from_down, rows_up, rows_down, after,
    a_e, a_w, a_n, a_s, a_c, m_e, m_w, m_n, m_s, m_c, head_out, ew_out, sw_out,
    square, side, nat, kring, cring,
):
    group = lax.axis_index("comp")
    has_up, has_down, has_left, has_right = edges_of_grid()

    @pl.when(group == 1)
    def _():
        lane128 = lax.broadcasted_iota(jnp.int32, (40, 128), 1)

        def column(own, down, up):
            down, up = pltpu.roll(down, 80, 1), pltpu.roll(up, 16, 1)
            return jnp.where(lane128 < 80, own, jnp.where(lane128 < 88, down * has_down, up * has_up))

        square[...] = jnp.zeros((128, 128), F32)
        square[0:40] = column(from_right[...], from_down[40:80], from_up[40:80]) * has_right
        square[64:104] = column(from_left[...], from_down[0:40], from_up[0:40]) * has_left
        side[...] = square[...].T
        own = (keff, head, code, ew, sw)
        lane = lax.broadcasted_iota(jnp.int32, (96, 128), 1)
        for f in range(FIELDS):
            for t in range(10):
                at = f * 80 + t * 8
                nat[t, 0:ROWS] = own[f][:, cut(t)]
                nat[t, ROWS : ROWS + 8] = rows_down[at : at + 8] * has_down
                nat[t, ROWS + 8 : ROWS + 16] = rows_up[at : at + 8] * has_up
            columns = side[0:96]
            right = columns if f == 0 else pltpu.roll(columns, (-8 * f) % 128, 1)
            left = pltpu.roll(columns, 120 - 64 - 8 * f, 1)
            nat[10] = jnp.where(lane < 8, right, jnp.where(lane >= 120, left, 0.0))
            for k in range(STRIPS):
                for t in range(TILES):
                    value = nat[t, pl.ds(k, 8, stride=STRIPS), :]
                    if f == 0:
                        kring[k + 1, :, cut(t)] = value
                    elif f == 1:
                        active = kring[k + 1, :, cut(t)] > 0.0
                        head_out[k, :, cut(t)] = jnp.where(active, value, 0.0)
                    elif f == 2:
                        cring[k + 1, :, cut(t)] = value
                    elif f == 3:
                        active = kring[k + 1, :, cut(t)] > 0.0
                        ew_out[k, :, cut(t)] = jnp.where(active, value, 0.0)
                    else:
                        sw_out[k, :, cut(t)] = value
        for ring in (kring, cring):
            for t in range(TILES):
                ring[0, :, cut(t)] = pltpu.roll(ring[STRIPS, :, cut(t)], 1, 0)
                ring[STRIPS + 1, :, cut(t)] = pltpu.roll(ring[1, :, cut(t)], 7, 0)

        def strip(k, carry):
            lane = lanes()
            here = [kring[k + 1, :, cut(t)] for t in range(TILES)]
            codes = [cring[k + 1, :, cut(t)] for t in range(TILES)]
            west, east = beside(here, lane)

            def drains(cond, codes, number):
                return jnp.where((cond > 0.0) & (codes == number), drainage_rate, 0.0)

            to_east, _ = beside([drains(here[t], codes[t], 3.0) for t in range(TILES)], lane)
            _, to_west = beside([drains(here[t], codes[t], 2.0) for t in range(TILES)], lane)
            for t in range(TILES):
                north, south = kring[k, :, cut(t)], kring[k + 2, :, cut(t)]
                n, s = jnp.sqrt(here[t] * north), jnp.sqrt(here[t] * south)
                w, e = jnp.sqrt(here[t] * west[t]), jnp.sqrt(here[t] * east[t])
                a_n[k, :, cut(t)] = n
                a_s[k, :, cut(t)] = s
                a_w[k, :, cut(t)] = w
                a_e[k, :, cut(t)] = e
                a_c[k, :, cut(t)] = 1.0 - ((n + s) + (w + e))
                m_n[k, :, cut(t)] = drains(north, cring[k, :, cut(t)], 1.0)
                m_s[k, :, cut(t)] = drains(south, cring[k + 2, :, cut(t)], 0.0)
                m_w[k, :, cut(t)] = to_east[t]
                m_e[k, :, cut(t)] = to_west[t]
                m_c[k, :, cut(t)] = jnp.where(here[t] > 0.0, drainage_rate, 0.0)
            return carry

        lax.fori_loop(0, STRIPS, strip, 0)


def route_kernel(
    coarse, a_e, a_w, a_n, a_s, a_c, m_e, m_w, m_n, m_s, m_c, head, ew, sw, up_cols, up_rows, pool_cols, pool_rows,
    ponded_out, stored_out, pond_a, pond_b, store_a, store_b,
):
    group = lax.axis_index("comp")

    @pl.when(group == 1)
    def _():
        pieces = jnp.concatenate([*split(coarse[0]), *split(coarse[1])], axis=0)
        wide = dot(pieces, up_cols[...]).astype(BF)
        excess = dot(up_rows[...], wide[0:32])
        moist = dot(up_rows[...], wide[32:64])
        pond_a[1 : STRIPS + 1] = head[...] + ew[...] * excess.reshape(STRIPS, 8, WIDE)
        store_a[1 : STRIPS + 1] = sw[...] * moist.reshape(STRIPS, 8, WIDE)

        def close(ring):
            for t in range(TILES):
                ring[0, :, cut(t)] = pltpu.roll(ring[STRIPS, :, cut(t)], 1, 0)
                ring[STRIPS + 1, :, cut(t)] = pltpu.roll(ring[1, :, cut(t)], 7, 0)

        close(pond_a)
        close(store_a)

        def substep(pond, store, new_pond, new_store):
            lane = lanes()
            first, last = lane == 0, lane == 127
            for k in range(STRIPS):
                p, s = pond[k + 1, :, cut(0)], store[k + 1, :, cut(0)]
                q = s * s
                p_left, q_left = pltpu.roll(p, 127, 1), pltpu.roll(q, 127, 1)
                s_r = store[k + 1, :, cut(TILES - 1)]
                p_before = pltpu.roll(pond[k + 1, :, cut(TILES - 1)], 1, 1)
                q_before = pltpu.roll(s_r * s_r, 1, 1)
                for t in range(TILES):
                    c, after = cut(t), cut((t + 1) % TILES)
                    p_next, s_next = pond[k + 1, :, after], store[k + 1, :, after]
                    q_next = s_next * s_next
                    p_right, q_right = pltpu.roll(p, 1, 1), pltpu.roll(q, 1, 1)
                    p_next_left, q_next_left = pltpu.roll(p_next, 127, 1), pltpu.roll(q_next, 127, 1)
                    p_w, p_e = jnp.where(first, p_before, p_right), jnp.where(last, p_next_left, p_left)
                    q_w, q_e = jnp.where(first, q_before, q_right), jnp.where(last, q_next_left, q_left)
                    s_n, s_s = store[k, :, c], store[k + 2, :, c]
                    below = 1.0 + s
                    guess = pltpu.reciprocal(below, approx=True)
                    guess = guess * (2.0 - below * guess)
                    soaked = infiltration_rate * p * guess
                    flow = a_n[k, :, c] * pond[k, :, c] + a_s[k, :, c] * pond[k + 2, :, c]
                    flow = flow + (a_w[k, :, c] * p_w + a_e[k, :, c] * p_e)
                    new_pond[k + 1, :, c] = a_c[k, :, c] * p + flow - soaked
                    inflow = m_n[k, :, c] * (s_n * s_n) + m_s[k, :, c] * (s_s * s_s)
                    inflow = inflow + (m_w[k, :, c] * q_w + m_e[k, :, c] * q_e)
                    new_store[k + 1, :, c] = s + soaked - m_c[k, :, c] * q + inflow
                    p, s, q, p_left, q_left = p_next, s_next, q_next, p_next_left, q_next_left
                    p_before, q_before = p_right, q_right
            close(new_pond)
            close(new_store)

        def two(i, carry):
            substep(pond_a, store_a, pond_b, store_b)
            substep(pond_b, store_b, pond_a, store_a)
            return carry

        lax.fori_loop(0, NSUB // 2, two, 0)
        for ring, out in ((pond_a, ponded_out), (store_a, stored_out)):
            high, low = split(ring[1 : STRIPS + 1].reshape(STRIPS * 8, WIDE))
            part = dot(high, pool_cols[...]) + dot(low, pool_cols[...])
            out[...] = dot(pool_rows[...], jnp.concatenate([*split(part)], axis=0)) * (1.0 / (AGG * AGG))


def moved(array, mesh_shape, target):
    groups, ys, xs = mesh_shape
    pairs = []
    for g in range(groups):
        for y in range(ys):
            for x in range(xs):
                a, b, c = target(g, y, x)
                pairs.append(((g * ys + y) * xs + x, ((a % groups) * ys + b % ys) * xs + c % xs))
    return lax.ppermute(array, ("comp", "gy", "gx"), pairs)


def f32(*shape):
    return jax.ShapeDtypeStruct(shape, F32)


def per_device(
    column_water,
    land_soil,
    level_weight,
    excess_weight,
    soil_weight,
    terrain_class,
    surface_head,
    conductivity,
    active_mask,
    flow_code,
):
    shape = tuple(lax.axis_size(axis) for axis in ("comp", "gy", "gx"))
    group = lax.axis_index("comp")
    m = tables()
    params = pltpu.CompilerParams(vmem_limit_bytes=32 * 1024 * 1024)
    arguments = (
        column_water[0].reshape(128, 128), land_soil[0], level_weight[None], excess_weight[None], soil_weight[None],
        terrain_class, surface_head[0], conductivity[0], active_mask[0], flow_code[0],
    )
    hbm = pl.BlockSpec(memory_space=pltpu.HBM)
    fine = f32(ROWS, COLS)
    fine_int = pltpu.VMEM((ROWS, COLS), jnp.int32)
    gxl, gxr, main_up, main_down, gyu, gyd, water, soil, weight, keff, head, code, ew, sw = pl.pallas_call(
        pack_kernel,
        in_specs=[hbm] * 10,
        out_shape=[f32(40, 128)] * 2
        + [f32(56, 128)] * 2
        + [f32(400, 128)] * 2
        + [f32(128, 128), f32(8, 128), f32(LEV, 128)]
        + [fine] * 5,
        scratch_shapes=[
            pltpu.VMEM((128, 128), F32),
            pltpu.VMEM((3, 1, NW), F32),
            fine_int,
            fine_int,
            fine_int,
            pltpu.SemaphoreType.DMA((2 + 5 * CHUNKS,)),
        ],
        compiler_params=params,
        name="pack",
    )(*(pltpu.with_memory_space_constraint(array, pltpu.HBM) for array in arguments))
    from_left = moved(gxr, shape, lambda g, y, x: (g, y, x + 1))
    from_right = moved(gxl, shape, lambda g, y, x: (g, y, x - 1))
    rows_up = moved(gyd, shape, lambda g, y, x: (g, y + 1, x) if g else (g, y, x ^ 1))
    rows_down = moved(gyu, shape, lambda g, y, x: (g, y - 1, x) if g else (g, y, x ^ 1))
    land = [from_left[:16], from_right[:16]]
    land_up = moved(jnp.concatenate(land + [main_down]), shape, lambda g, y, x: (g, y, x ^ 1) if g else (g, y + 1, x))
    land_down = moved(jnp.concatenate(land + [main_up]), shape, lambda g, y, x: (g, y, x ^ 1) if g else (g, y - 1, x))
    route = jnp.concatenate([from_left, from_right])
    route_up = moved(route, shape, lambda g, y, x: (g, y + 1, x) if g else (g, y, x ^ 1))
    route_down = moved(route, shape, lambda g, y, x: (g, y - 1, x) if g else (g, y, x ^ 1))
    coarse, water_top = pl.pallas_call(
        land_kernel,
        out_shape=[f32(2, 16, 256), f32(8, 128)],
        scratch_shapes=[pltpu.VMEM((128, 128), F32), pltpu.VMEM((3, 128, 128), F32)],
        compiler_params=params,
        name="land",
    )(water, soil, weight, from_left, from_right, land_up, land_down)
    arrived = moved(coarse, shape, lambda g, y, x: (1 - g, y, x))
    strips = f32(STRIPS, 8, WIDE)
    ring = pltpu.VMEM((STRIPS + 2, 8, WIDE), F32)
    prepared = pl.pallas_call(
        prepare_kernel,
        out_shape=[strips] * 13,
        scratch_shapes=[
            pltpu.VMEM((128, 128), F32),
            pltpu.VMEM((128, 128), F32),
            pltpu.VMEM((TILES, 96, 128), F32),
            ring,
            ring,
        ],
        compiler_params=params,
        name="prepare",
    )(keff, head, code, ew, sw, from_left, from_right, route_up, route_down, rows_up, rows_down, water_top)
    ring = pltpu.VMEM((STRIPS + 2, 8, WIDE), F32)
    ponded, stored = pl.pallas_call(
        route_kernel,
        out_shape=[f32(8, 128), f32(8, 128)],
        scratch_shapes=[ring] * 4,
        compiler_params=params,
        name="route",
    )(arrived, *prepared, m["up_cols"], m["up_rows"], m["pool_cols"], m["pool_rows"])
    returned = moved(stored, shape, lambda g, y, x: (1 - g, y, x))
    land_out = returned / (1.0 + evaporation_scale * water_top * water_top)
    return jnp.where(group == 0, land_out, ponded)[None]


def solution(mesh):
    in_specs = (
        P("comp", None, "gy", "gx"),
        P("comp", "gy", "gx"),
        P(),
        P(),
        P(),
        P("gy", "gx"),
        P("comp", "gy", "gx"),
        P("comp", "gy", "gx"),
        P("comp", "gy", "gx"),
        P("comp", "gy", "gx"),
    )
    out_specs = P("comp", "gy", "gx")
    return jax.shard_map(
        per_device, mesh=mesh, in_specs=in_specs, out_specs=out_specs, check_vma=False
    )
```

```python
import jax
import jax.numpy as jnp
from jax import lax
from jax.experimental import pallas as pl
from jax.experimental.pallas import tpu as pltpu
from jax.sharding import PartitionSpec as P

AGG = 10
NSUB = 8
LEV = 16
ROWS = 80
COLS = 1280
HALO = 8
STRIPS = 12
TILES = 11
WIDE = TILES * 128
CHUNKS = 1
NW = 16
BF = jnp.bfloat16
F32 = jnp.float32

diffusion_rate = 0.2
infiltration_rate = 0.05
drainage_rate = 0.1
half_point = 0.1
evaporation_scale = 0.5


def split(x):
    high = x.astype(BF)
    return high, (x - high.astype(F32)).astype(BF)


def dot(a, b):
    return jnp.dot(a, b, preferred_element_type=F32)


def both(x):
    return jnp.concatenate(split(x), axis=0)


def inverse(total):
    return float(AGG * AGG) / jnp.where(total > 0.0, total, 1.0)


def twice(x):
    return jnp.concatenate([x, x], axis=1)


def lanes():
    return lax.broadcasted_iota(jnp.int32, (8, 128), 1)


def beside(tiles, lane):
    right = [pltpu.roll(x, 1, 1) for x in tiles]
    left = [pltpu.roll(x, 127, 1) for x in tiles]
    n = len(tiles)
    west = [jnp.where(lane == 0, right[t - 1], right[t]) for t in range(n)]
    east = [jnp.where(lane == 127, left[(t + 1) % n], left[t]) for t in range(n)]
    return west, east


def cut(t):
    return slice(t * 128, (t + 1) * 128)


def within(shape, fine_axis):
    fine = lax.broadcasted_iota(jnp.int32, shape, fine_axis)
    first = AGG * lax.broadcasted_iota(jnp.int32, shape, 1 - fine_axis)
    return jnp.where((fine >= first) & (fine < first + AGG), 1.0, 0.0).astype(BF)


def pack_kernel(
    water_in, soil_in, weight_in, etab_in, stab_in, terrain_in, head_in, cond_in, mask_in, code_in,
    gxl, gxr, main_up, main_down, gyu, gyd, water, soil, weight, tabs, terrain, keff, head, code,
    square, mask, code_int, sems,
):
    group = lax.axis_index("comp")

    @pl.when(group == 0)
    def _():
        loads = [
            pltpu.make_async_copy(water_in, water, sems.at[0]),
            pltpu.make_async_copy(soil_in, soil, sems.at[1]),
            pltpu.make_async_copy(weight_in, tabs.at[0], sems.at[2]),
        ]
        for load in loads:
            load.start()
        gxl[16:40] = jnp.zeros((24, 128), F32)
        gxr[16:40] = jnp.zeros((24, 128), F32)
        square[16:128] = jnp.zeros((112, 128), F32)
        for load in loads:
            load.wait()
        square[0:8] = soil[...]
        square[8:9, 0:LEV] = tabs[0]
        turned = square[...].T
        gxl[8:16] = turned[0:8]
        gxr[8:16] = turned[120:128]
        weight[...] = jnp.broadcast_to(turned[0:LEV, 8:9], (LEV, 128))
        square[...] = water[...].T
        gxl[0:8] = square[0:8]
        gxr[0:8] = square[120:128]
        for j in range(3):
            for h in range(2):
                at = j * 16 + h * 8
                main_up[at : at + 8] = water[pl.ds(h * 64 + j, 8, stride=8), :]
                main_down[at : at + 8] = water[pl.ds(h * 64 + 5 + j, 8, stride=8), :]
        main_up[48:56] = soil[...]
        main_down[48:56] = soil[...]

    @pl.when(group == 1)
    def _():
        load_tabs = [
            pltpu.make_async_copy(etab_in, tabs.at[1], sems.at[0]),
            pltpu.make_async_copy(stab_in, tabs.at[2], sems.at[1]),
        ]
        loads = []
        for i, (source, target) in enumerate(
            ((terrain_in, terrain), (cond_in, keff), (mask_in, mask), (head_in, head), (code_in, code_int))
        ):
            parts = []
            for j in range(CHUNKS):
                rows = pl.ds(j * (ROWS // CHUNKS), ROWS // CHUNKS)
                parts.append(pltpu.make_async_copy(source.at[rows], target.at[rows], sems.at[2 + i * CHUNKS + j]))
                parts[-1].start()
            loads.append(parts)

        for load in load_tabs:
            load.start()

        def ready(i):
            for part in loads[i]:
                part.wait()

        ready(1)
        ready(2)
        keff[...] = keff[...] * mask[...].astype(F32)
        ready(4)
        code[...] = code_int[...].astype(F32)
        ready(3)
        ready(0)

        def terrain_at(r, c):
            return terrain[r, c].astype(F32)

        fields = (lambda r, c: keff[r, c], lambda r, c: head[r, c], lambda r, c: code[r, c], terrain_at)
        for f, field in enumerate(fields):
            for t in range(10):
                at = f * 80 + t * 8
                gyu[at : at + 8] = field(slice(0, 8), cut(t))
                gyd[at : at + 8] = field(slice(ROWS - 8, ROWS), cut(t))
        for t in range(10):
            at = 320 + 2 * t
            gyu[at : at + 2] = terrain_at(slice(8, 10), cut(t))
            gyd[at : at + 2] = terrain_at(slice(ROWS - 10, ROWS - 8), cut(t))
        gyu[340:344] = jnp.zeros((4, 128), F32)
        gyd[340:344] = jnp.zeros((4, 128), F32)
        lane = lax.broadcasted_iota(jnp.int32, (ROWS, 128), 1)
        edges = jnp.zeros((ROWS, 128), F32)
        for f, field in enumerate(fields):
            width = 8 if f < 3 else AGG
            first = field(slice(0, ROWS), cut(0))
            last = field(slice(0, ROWS), cut(9))
            first = first if f == 0 else pltpu.roll(first, 8 * f, 1)
            last = pltpu.roll(last, (64 + 8 * f + width) % 128, 1)
            edges = jnp.where((lane >= 8 * f) & (lane < 8 * f + width), first, edges)
            edges = jnp.where((lane >= 64 + 8 * f) & (lane < 64 + 8 * f + width), last, edges)
        square[0:ROWS] = edges
        square[ROWS:128] = jnp.zeros((128 - ROWS, 128), F32)
        square[...] = square[...].T
        gxl[...] = square[0:40]
        gxr[...] = square[64:104]
        for load in load_tabs:
            load.wait()


def table_rows(tabs, i):
    return jnp.concatenate([jnp.broadcast_to(tabs[i], (8, NW))] * (128 // NW), axis=1)


def ratio_kernel(tabs, terrain, ew, sw, up_cols, pool_cols, up_rows, pool_rows, found):
    group = lax.axis_index("comp")

    @pl.when(group == 1)
    def _():
        def columns(shape, fine_axis):
            fine = lax.broadcasted_iota(jnp.int32, shape, fine_axis)
            coarse = lax.broadcasted_iota(jnp.int32, shape, 1 - fine_axis)
            first = jnp.where(coarse == 255, WIDE - AGG, jnp.where(coarse <= 128, AGG * coarse, 2 * WIDE))
            return jnp.where((fine >= first) & (fine < first + AGG), 1.0, 0.0).astype(BF)

        up_cols[...] = columns((256, WIDE), 1)
        pool_cols[...] = columns((WIDE, 256), 0)

        def fine_rows(shape, axis):
            at = lax.broadcasted_iota(jnp.int32, shape, axis)
            at = jnp.where(at >= 96, at - 96, at)
            strip = lax.shift_right_logical(at, 3)
            return STRIPS * (at - 8 * strip) + strip

        fine, coarse = fine_rows((192, 64), 0), lax.broadcasted_iota(jnp.int32, (192, 64), 1)
        lower = lax.broadcasted_iota(jnp.int32, (192, 64), 0) >= 96
        mine = jnp.where(coarse >= 32, 1, 0) == jnp.where(lower, 1, 0)
        coarse = lax.rem(coarse, 16)
        own = (fine >= AGG * coarse) & (fine < AGG * coarse + AGG) & (coarse < 8)
        below = (fine >= ROWS) & (fine < ROWS + 8) & (coarse == 8)
        above = (fine >= ROWS + 8) & (coarse == 15)
        up_rows[...] = jnp.where(mine & (own | below | above), 1.0, 0.0).astype(BF)
        fine, coarse = fine_rows((8, 192), 1), lax.broadcasted_iota(jnp.int32, (8, 192), 0)
        pool_rows[...] = jnp.where((fine >= AGG * coarse) & (fine < AGG * coarse + AGG), 1.0, 0.0).astype(BF)

        for i in range(2):
            table = table_rows(tabs, 1 + i)
            for r in range(0, ROWS, 8):
                for t in range(10):
                    found[i * ROWS + r : i * ROWS + r + 8, cut(t)] = jnp.take_along_axis(
                        table, terrain[r : r + 8, cut(t)], axis=1
                    )
        part = dot(both(found[...]), pool_cols[0:COLS, 0:128])
        part = part[0:160] + part[160:320]
        part = jnp.concatenate([part[0:ROWS], part[ROWS:160]], axis=1)
        total = dot(twice(within((8, ROWS), 1)), both(part))
        scale = inverse(total)
        scale = jnp.concatenate([both(scale[:, 0:128]), both(scale[:, 128:256])], axis=0)
        wide = dot(scale, up_cols[0:128, 0:COLS]).astype(BF)
        repeat = twice(within((ROWS, 8), 0))
        ew[...] = found[0:ROWS] * dot(repeat, wide[0:16])
        sw[...] = found[ROWS:160] * dot(repeat, wide[16:32])


def edges_of_grid():
    gy, gx = lax.axis_index("gy"), lax.axis_index("gx")
    has_up = (gy > 0).astype(F32)
    has_down = (gy < lax.axis_size("gy") - 1).astype(F32)
    has_left = (gx > 0).astype(F32)
    has_right = (gx < lax.axis_size("gx") - 1).astype(F32)
    return has_up, has_down, has_left, has_right


def land_kernel(
    water, soil, weight, from_left, from_right, from_up, from_down, coarse, water_out, square, side,
):
    group = lax.axis_index("comp")
    has_up, has_down, has_left, has_right = edges_of_grid()

    @pl.when(group == 0)
    def _():
        pairs = (
            (from_right[0:8], from_left[0:8]),
            (from_down[16:24], from_down[0:8]),
            (from_up[16:24], from_up[0:8]),
        )
        square[8:120] = jnp.zeros((112, 128), F32)
        for i, (right, left) in enumerate(pairs):
            square[0:8] = right
            square[120:128] = left
            side[i] = square[...].T
        lane = lanes()
        for at, (own, down, up) in (
            (0, (from_right[8:16], from_down[24:32], from_up[24:32])),
            (120, (from_left[8:16], from_down[8:16], from_up[8:16])),
        ):
            square[at : at + 8] = jnp.where(
                lane < 8, own, jnp.where(lane < 16, pltpu.roll(down, 8, 1), pltpu.roll(up, 16, 1))
            )
        side_soil = square[...].T

        lane2 = lax.broadcasted_iota(jnp.int32, (1, 256), 1)
        col_ok = jnp.where(lane2 < 128, 1.0, jnp.where(lane2 < 192, has_right, has_left))

        def levels(ref, row):
            return jnp.concatenate(
                [ref[pl.ds(h * 64 + row, 8, stride=8), :] for h in range(2)], axis=0
            )

        def side_levels(i, row):
            return jnp.concatenate(
                [side[i, pl.ds(h * 64 + row, 8, stride=8), :] for h in range(2)], axis=0
            )

        field = []
        for j in range(3):
            tile = from_up[32 + j * 16 : 48 + j * 16]
            field.append(jnp.concatenate([tile, side_levels(2, 5 + j)], axis=1) * (col_ok * has_up))
        for j in range(8):
            field.append(jnp.concatenate([levels(water, j), side_levels(0, j)], axis=1) * col_ok)
        for j in range(3):
            tile = from_down[32 + j * 16 : 48 + j * 16]
            field.append(jnp.concatenate([tile, side_levels(1, j)], axis=1) * (col_ok * has_down))

        def sweep(old, first, last):
            new = {}
            for q in range(first, last):
                around = old[q - 1] + old[q + 1] + pltpu.roll(old[q], 1, 1) + pltpu.roll(old[q], 255, 1)
                new[q] = old[q] + diffusion_rate * (around - 4.0 * old[q])
            return new

        once = sweep(field, 1, 13)
        for q in once:
            once[q] = once[q] * (col_ok * (has_up if q < 3 else has_down if q > 10 else 1.0))
        twice = sweep(once, 2, 12)
        for j in range(8):
            water_out[j : j + 1] = twice[3 + j][0:1, 0:128]
        level_weight = jnp.concatenate([weight[...]] * 2, axis=1)
        rain = {q: jnp.sum(level_weight * twice[q] * twice[q], axis=0, keepdims=True) for q in twice}
        blank = jnp.zeros((6, 256), F32)
        rain = jnp.concatenate([rain[3 + j] for j in range(8)] + [rain[11], blank, rain[2]], axis=0)
        moist = jnp.concatenate(
            [
                jnp.concatenate([soil[...], side_soil[0:8]], axis=1),
                jnp.concatenate([from_down[80:81], side_soil[8:9]], axis=1),
                blank,
                jnp.concatenate([from_up[87:88], side_soil[23:24]], axis=1),
            ],
            axis=0,
        )
        coarse[0] = rain * moist * moist / (moist * moist + half_point)
        coarse[1] = moist


def prepare_kernel(
    keff, head, code, ew, sw, tabs, up_cols, pool_cols, from_left, from_right, from_up, from_down, rows_up, rows_down, after,
    a_e, a_w, a_n, a_s, a_c, m_e, m_w, m_n, m_s, m_c, head_out, ew_out, sw_out,
    square, side, nat, kring, cring, outer, found, near,
):
    group = lax.axis_index("comp")
    has_up, has_down, has_left, has_right = edges_of_grid()

    @pl.when(group == 1)
    def _():
        lane128 = lax.broadcasted_iota(jnp.int32, (40, 128), 1)

        def column(own, down, up):
            down, up = pltpu.roll(down, 80, 1), pltpu.roll(up, 24, 1)
            return jnp.where(lane128 < 80, own, jnp.where(lane128 < 92, down * has_down, up * has_up))

        square[...] = jnp.zeros((128, 128), F32)
        square[0:40] = column(from_right[...], from_down[40:80], from_up[40:80]) * has_right
        square[64:104] = column(from_left[...], from_down[0:40], from_up[0:40]) * has_left
        side[...] = square[...].T
        lane = lax.broadcasted_iota(jnp.int32, (104, 128), 1)

        def columns_of(f, width):
            right = side[0:104] if f == 0 else pltpu.roll(side[0:104], (-8 * f) % 128, 1)
            left = pltpu.roll(side[0:104], (64 - 8 * f - width) % 128, 1)
            return jnp.where(lane < width, right, jnp.where(lane >= 128 - width, left, 0.0))

        def interleave(f):
            for k in range(STRIPS):
                for t in range(TILES):
                    value = nat[t, pl.ds(k, 8, stride=STRIPS), :]
                    if f == 0:
                        kring[k + 1, :, cut(t)] = value
                    elif f == 1:
                        active = kring[k + 1, :, cut(t)] > 0.0
                        head_out[k, :, cut(t)] = jnp.where(active, value, 0.0)
                    elif f == 2:
                        cring[k + 1, :, cut(t)] = value
                    elif f == 3:
                        active = kring[k + 1, :, cut(t)] > 0.0
                        ew_out[k, :, cut(t)] = jnp.where(active, value, 0.0)
                    else:
                        sw_out[k, :, cut(t)] = value

        for f, own in enumerate((keff, head, code)):
            for t in range(10):
                at = f * 80 + t * 8
                nat[t, 0:ROWS] = own[:, cut(t)]
                nat[t, ROWS : ROWS + 8] = rows_down[at : at + 8] * has_down
                nat[t, ROWS + 8 : ROWS + 16] = rows_up[at : at + 8] * has_up
            columns = columns_of(f, 8)
            nat[10, 0 : ROWS + 8] = columns[0 : ROWS + 8]
            nat[10, ROWS + 8 : ROWS + 16] = columns[96:104]
            interleave(f)

        corner = columns_of(3, AGG)
        outer[...] = jnp.zeros((32, WIDE), F32)
        for at, rows in ((0, rows_down), (16, rows_up)):
            for t in range(10):
                outer[at : at + 8, cut(t)] = rows[240 + t * 8 : 248 + t * 8]
                outer[at + 8 : at + 10, cut(t)] = rows[320 + t * 2 : 322 + t * 2]
        outer[0:10, cut(10)] = corner[80:90]
        outer[16:24, cut(10)] = corner[96:104]
        outer[24:26, cut(10)] = corner[94:96]
        square[0:ROWS] = corner[0:ROWS]
        for i in range(2):
            table = table_rows(tabs, 1 + i)
            for r in range(0, 32, 8):
                for t in range(TILES):
                    found[i * 32 + r : i * 32 + r + 8, cut(t)] = jnp.take_along_axis(
                        table, outer[r : r + 8, cut(t)].astype(jnp.int32), axis=1
                    )
            for r in range(0, ROWS, 8):
                near[i * ROWS + r : i * ROWS + r + 8] = jnp.take_along_axis(
                    table, square[r : r + 8].astype(jnp.int32), axis=1
                )
        part = dot(both(found[...]), pool_cols[...])
        part = part[0:64] + part[64:128]
        totals = []
        for at in (0, 16, 32, 48):
            totals.append(jnp.sum(part[at : at + 8], axis=0, keepdims=True) + part[at + 8 : at + 9] + part[at + 9 : at + 10])
        scale = inverse(jnp.concatenate(totals + [jnp.zeros((4, 256), F32)], axis=0))
        wide = dot(both(scale), up_cols[...])
        wide = wide[0:8] + wide[8:16]

        col = lax.broadcasted_iota(jnp.int32, (128, 128), 1)
        row = lax.broadcasted_iota(jnp.int32, (128, 128), 0)
        ends = jnp.where(((col == 0) & (row < AGG)) | ((col == 1) & (row >= 128 - AGG)), 1.0, 0.0).astype(BF)
        part = dot(both(near[...]), ends)
        part = part[0:160] + part[160:320]
        part = jnp.concatenate([part[0:ROWS], part[ROWS:160]], axis=1)
        scale = inverse(dot(twice(within((8, ROWS), 1)), both(part)))
        scale = dot(twice(within((ROWS, 8), 0)), both(scale))
        first = lax.broadcasted_iota(jnp.int32, (ROWS, 128), 1) < AGG
        for i, own in enumerate((ew, sw)):
            for t in range(TILES):
                nat[t, ROWS : ROWS + 8] = found[32 * i : 32 * i + 8, cut(t)] * wide[2 * i : 2 * i + 1, cut(t)]
                nat[t, ROWS + 8 : ROWS + 16] = (
                    found[32 * i + 16 : 32 * i + 24, cut(t)] * wide[2 * i + 1 : 2 * i + 2, cut(t)]
                )
            at = 128 * i
            nat[10, 0:ROWS] = near[i * ROWS : (i + 1) * ROWS] * jnp.where(
                first, scale[:, at : at + 1], scale[:, at + 1 : at + 2]
            )
            for t in range(10):
                nat[t, 0:ROWS] = own[:, cut(t)]
            interleave(3 + i)
        for ring in (kring, cring):
            for t in range(TILES):
                ring[0, :, cut(t)] = pltpu.roll(ring[STRIPS, :, cut(t)], 1, 0)
                ring[STRIPS + 1, :, cut(t)] = pltpu.roll(ring[1, :, cut(t)], 7, 0)

        def strip(k, carry):
            lane = lanes()
            here = [kring[k + 1, :, cut(t)] for t in range(TILES)]
            codes = [cring[k + 1, :, cut(t)] for t in range(TILES)]
            west, east = beside(here, lane)

            def drains(cond, codes, number):
                return jnp.where((cond > 0.0) & (codes == number), drainage_rate, 0.0)

            to_east, _ = beside([drains(here[t], codes[t], 3.0) for t in range(TILES)], lane)
            _, to_west = beside([drains(here[t], codes[t], 2.0) for t in range(TILES)], lane)
            for t in range(TILES):
                north, south = kring[k, :, cut(t)], kring[k + 2, :, cut(t)]
                n, s = jnp.sqrt(here[t] * north), jnp.sqrt(here[t] * south)
                w, e = jnp.sqrt(here[t] * west[t]), jnp.sqrt(here[t] * east[t])
                a_n[k, :, cut(t)] = n
                a_s[k, :, cut(t)] = s
                a_w[k, :, cut(t)] = w
                a_e[k, :, cut(t)] = e
                a_c[k, :, cut(t)] = 1.0 - ((n + s) + (w + e))
                m_n[k, :, cut(t)] = drains(north, cring[k, :, cut(t)], 1.0)
                m_s[k, :, cut(t)] = drains(south, cring[k + 2, :, cut(t)], 0.0)
                m_w[k, :, cut(t)] = to_east[t]
                m_e[k, :, cut(t)] = to_west[t]
                m_c[k, :, cut(t)] = jnp.where(here[t] > 0.0, drainage_rate, 0.0)
            return carry

        lax.fori_loop(0, STRIPS, strip, 0)


def route_kernel(
    coarse, a_e, a_w, a_n, a_s, a_c, m_e, m_w, m_n, m_s, m_c, head, ew, sw, up_cols, up_rows, pool_cols, pool_rows,
    ponded_out, stored_out, pond_a, pond_b, store_a, store_b,
):
    group = lax.axis_index("comp")

    @pl.when(group == 1)
    def _():
        pieces = jnp.concatenate([*split(coarse[0]), *split(coarse[1])], axis=0)
        fields = dot(up_rows[...], dot(pieces, up_cols[...]).astype(BF))
        excess, moist = fields[0:96], fields[96:192]
        pond_a[1 : STRIPS + 1] = head[...] + ew[...] * excess.reshape(STRIPS, 8, WIDE)
        store_a[1 : STRIPS + 1] = sw[...] * moist.reshape(STRIPS, 8, WIDE)

        def close(ring):
            for t in range(TILES):
                ring[0, :, cut(t)] = pltpu.roll(ring[STRIPS, :, cut(t)], 1, 0)
                ring[STRIPS + 1, :, cut(t)] = pltpu.roll(ring[1, :, cut(t)], 7, 0)

        close(pond_a)
        close(store_a)

        def substep(pond, store, new_pond, new_store):
            lane = lanes()
            first, last = lane == 0, lane == 127
            for k in range(STRIPS):
                p, s = pond[k + 1, :, cut(0)], store[k + 1, :, cut(0)]
                q = s * s
                p_left, q_left = pltpu.roll(p, 127, 1), pltpu.roll(q, 127, 1)
                s_r = store[k + 1, :, cut(TILES - 1)]
                p_before = pltpu.roll(pond[k + 1, :, cut(TILES - 1)], 1, 1)
                q_before = pltpu.roll(s_r * s_r, 1, 1)
                for t in range(TILES):
                    c, after = cut(t), cut((t + 1) % TILES)
                    p_next, s_next = pond[k + 1, :, after], store[k + 1, :, after]
                    q_next = s_next * s_next
                    p_right, q_right = pltpu.roll(p, 1, 1), pltpu.roll(q, 1, 1)
                    p_next_left, q_next_left = pltpu.roll(p_next, 127, 1), pltpu.roll(q_next, 127, 1)
                    p_w, p_e = jnp.where(first, p_before, p_right), jnp.where(last, p_next_left, p_left)
                    q_w, q_e = jnp.where(first, q_before, q_right), jnp.where(last, q_next_left, q_left)
                    s_n, s_s = store[k, :, c], store[k + 2, :, c]
                    below = 1.0 + s
                    guess = pltpu.reciprocal(below, approx=True)
                    guess = guess * (2.0 - below * guess)
                    soaked = infiltration_rate * p * guess
                    flow = a_n[k, :, c] * pond[k, :, c] + a_s[k, :, c] * pond[k + 2, :, c]
                    flow = flow + (a_w[k, :, c] * p_w + a_e[k, :, c] * p_e)
                    new_pond[k + 1, :, c] = a_c[k, :, c] * p + flow - soaked
                    inflow = m_n[k, :, c] * (s_n * s_n) + m_s[k, :, c] * (s_s * s_s)
                    inflow = inflow + (m_w[k, :, c] * q_w + m_e[k, :, c] * q_e)
                    new_store[k + 1, :, c] = s + soaked - m_c[k, :, c] * q + inflow
                    p, s, q, p_left, q_left = p_next, s_next, q_next, p_next_left, q_next_left
                    p_before, q_before = p_right, q_right
            close(new_pond)
            close(new_store)

        def two(i, carry):
            substep(pond_a, store_a, pond_b, store_b)
            substep(pond_b, store_b, pond_a, store_a)
            return carry

        lax.fori_loop(0, NSUB // 2, two, 0)
        pieces = []
        for ring in (pond_a, store_a):
            pieces.extend(split(ring[1 : STRIPS + 1].reshape(STRIPS * 8, WIDE)))
        part = dot(jnp.concatenate(pieces, axis=0), pool_cols[:, 0:128])
        part = jnp.concatenate([part[0:96] + part[96:192], part[192:288] + part[288:384]], axis=1)
        mean = dot(pool_rows[...], both(part)) * (1.0 / (AGG * AGG))
        ponded_out[...] = mean[:, 0:128]
        stored_out[...] = mean[:, 128:256]


def moved(array, mesh_shape, target):
    groups, ys, xs = mesh_shape
    pairs = []
    for g in range(groups):
        for y in range(ys):
            for x in range(xs):
                a, b, c = target(g, y, x)
                pairs.append(((g * ys + y) * xs + x, ((a % groups) * ys + b % ys) * xs + c % xs))
    return lax.ppermute(array, ("comp", "gy", "gx"), pairs)


def f32(*shape):
    return jax.ShapeDtypeStruct(shape, F32)


def per_device(
    column_water,
    land_soil,
    level_weight,
    excess_weight,
    soil_weight,
    terrain_class,
    surface_head,
    conductivity,
    active_mask,
    flow_code,
):
    shape = tuple(lax.axis_size(axis) for axis in ("comp", "gy", "gx"))
    group = lax.axis_index("comp")
    params = pltpu.CompilerParams(vmem_limit_bytes=32 * 1024 * 1024)
    arguments = (
        column_water[0].reshape(128, 128), land_soil[0], level_weight[None], excess_weight[None], soil_weight[None],
        terrain_class, surface_head[0], conductivity[0], active_mask[0], flow_code[0],
    )
    hbm = pl.BlockSpec(memory_space=pltpu.HBM)
    fine = f32(ROWS, COLS)
    fine_int = pltpu.VMEM((ROWS, COLS), jnp.int32)
    gxl, gxr, main_up, main_down, gyu, gyd, water, soil, weight, tabs, terrain, keff, head, code = pl.pallas_call(
        pack_kernel,
        in_specs=[hbm] * 10,
        out_shape=[f32(40, 128)] * 2
        + [f32(56, 128)] * 2
        + [f32(344, 128)] * 2
        + [f32(128, 128), f32(8, 128), f32(LEV, 128), f32(3, 1, NW)]
        + [jax.ShapeDtypeStruct((ROWS, COLS), jnp.int32)]
        + [fine] * 3,
        scratch_shapes=[
            pltpu.VMEM((128, 128), F32),
            fine_int,
            fine_int,
            pltpu.SemaphoreType.DMA((2 + 5 * CHUNKS,)),
        ],
        compiler_params=params,
        name="pack",
    )(*(pltpu.with_memory_space_constraint(array, pltpu.HBM) for array in arguments))
    ew, sw, up_cols, pool_cols, up_rows, pool_rows = pl.pallas_call(
        ratio_kernel,
        out_shape=[fine] * 2
        + [jax.ShapeDtypeStruct(dims, BF) for dims in ((256, WIDE), (WIDE, 256), (192, 64), (8, 192))],
        scratch_shapes=[pltpu.VMEM((2 * ROWS, COLS), F32)],
        compiler_params=params,
        name="ratio",
    )(tabs, terrain)
    from_left = moved(gxr, shape, lambda g, y, x: (g, y, x + 1))
    from_right = moved(gxl, shape, lambda g, y, x: (g, y, x - 1))
    rows_up = moved(gyd, shape, lambda g, y, x: (g, y + 1, x) if g else (g, y, x ^ 1))
    rows_down = moved(gyu, shape, lambda g, y, x: (g, y - 1, x) if g else (g, y, x ^ 1))
    land = [from_left[:16], from_right[:16]]
    land_up = moved(jnp.concatenate(land + [main_down]), shape, lambda g, y, x: (g, y, x ^ 1) if g else (g, y + 1, x))
    land_down = moved(jnp.concatenate(land + [main_up]), shape, lambda g, y, x: (g, y, x ^ 1) if g else (g, y - 1, x))
    route = jnp.concatenate([from_left, from_right])
    route_up = moved(route, shape, lambda g, y, x: (g, y + 1, x) if g else (g, y, x ^ 1))
    route_down = moved(route, shape, lambda g, y, x: (g, y - 1, x) if g else (g, y, x ^ 1))
    coarse, water_top = pl.pallas_call(
        land_kernel,
        out_shape=[f32(2, 16, 256), f32(8, 128)],
        scratch_shapes=[pltpu.VMEM((128, 128), F32), pltpu.VMEM((3, 128, 128), F32)],
        compiler_params=params,
        name="land",
    )(water, soil, weight, from_left, from_right, land_up, land_down)
    arrived = moved(coarse, shape, lambda g, y, x: (1 - g, y, x))
    strips = f32(STRIPS, 8, WIDE)
    ring = pltpu.VMEM((STRIPS + 2, 8, WIDE), F32)
    prepared = pl.pallas_call(
        prepare_kernel,
        out_shape=[strips] * 13,
        scratch_shapes=[
            pltpu.VMEM((128, 128), F32),
            pltpu.VMEM((128, 128), F32),
            pltpu.VMEM((TILES, 96, 128), F32),
            ring,
            ring,
            pltpu.VMEM((32, WIDE), F32),
            pltpu.VMEM((64, WIDE), F32),
            pltpu.VMEM((2 * ROWS, 128), F32),
        ],
        compiler_params=params,
        name="prepare",
    )(
        keff, head, code, ew, sw, tabs, up_cols, pool_cols, from_left, from_right, route_up, route_down,
        rows_up, rows_down, water_top,
    )
    ring = pltpu.VMEM((STRIPS + 2, 8, WIDE), F32)
    ponded, stored = pl.pallas_call(
        route_kernel,
        out_shape=[f32(8, 128), f32(8, 128)],
        scratch_shapes=[ring] * 4,
        compiler_params=params,
        name="route",
    )(arrived, *prepared, up_cols, up_rows, pool_cols, pool_rows)
    returned = moved(stored, shape, lambda g, y, x: (1 - g, y, x))
    land_out = returned / (1.0 + evaporation_scale * water_top * water_top)
    return jnp.where(group == 0, land_out, ponded)[None]


def solution(mesh):
    in_specs = (
        P("comp", None, "gy", "gx"),
        P("comp", "gy", "gx"),
        P(),
        P(),
        P(),
        P("gy", "gx"),
        P("comp", "gy", "gx"),
        P("comp", "gy", "gx"),
        P("comp", "gy", "gx"),
        P("comp", "gy", "gx"),
    )
    out_specs = P("comp", "gy", "gx")
    return jax.shard_map(
        per_device, mesh=mesh, in_specs=in_specs, out_specs=out_specs, check_vma=False
    )
```

```python
import jax
import jax.numpy as jnp
from jax import lax
from jax.experimental import pallas as pl
from jax.experimental.pallas import tpu as pltpu
from jax.sharding import PartitionSpec as P

AGG = 10
NSUB = 8
LEV = 16
ROWS = 80
COLS = 1280
HALO = 8
STRIPS = 12
TILES = 11
WIDE = TILES * 128
CHUNKS = 1
NW = 16
BF = jnp.bfloat16
F32 = jnp.float32

diffusion_rate = 0.2
infiltration_rate = 0.05
drainage_rate = 0.1
half_point = 0.1
evaporation_scale = 0.5
SCALE = 1.0 / infiltration_rate


def split(x):
    high = x.astype(BF)
    return high, (x - high.astype(F32)).astype(BF)


def dot(a, b):
    return jnp.dot(a, b, preferred_element_type=F32)


def both(x):
    return jnp.concatenate(split(x), axis=0)


def inverse(total):
    return float(AGG * AGG) / jnp.where(total > 0.0, total, 1.0)


def twice(x):
    return jnp.concatenate([x, x], axis=1)


def lanes():
    return lax.broadcasted_iota(jnp.int32, (8, 128), 1)


def beside(tiles, lane):
    right = [pltpu.roll(x, 1, 1) for x in tiles]
    left = [pltpu.roll(x, 127, 1) for x in tiles]
    n = len(tiles)
    west = [jnp.where(lane == 0, right[t - 1], right[t]) for t in range(n)]
    east = [jnp.where(lane == 127, left[(t + 1) % n], left[t]) for t in range(n)]
    return west, east


def cut(t):
    return slice(t * 128, (t + 1) * 128)


def within(shape, fine_axis):
    fine = lax.broadcasted_iota(jnp.int32, shape, fine_axis)
    first = AGG * lax.broadcasted_iota(jnp.int32, shape, 1 - fine_axis)
    return jnp.where((fine >= first) & (fine < first + AGG), 1.0, 0.0).astype(BF)


def pack_kernel(
    water_in, soil_in, weight_in, etab_in, stab_in, terrain_in, head_in, cond_in, mask_in, code_in,
    gxl, gxr, main_up, main_down, gyu, gyd, water, soil, weight, tabs, terrain, keff, head, code,
    square, mask, code_int, sems,
):
    group = lax.axis_index("comp")

    @pl.when(group == 0)
    def _():
        loads = [
            pltpu.make_async_copy(water_in, water, sems.at[0]),
            pltpu.make_async_copy(soil_in, soil, sems.at[1]),
            pltpu.make_async_copy(weight_in, tabs.at[0], sems.at[2]),
        ]
        for load in loads:
            load.start()
        gxl[...] = jnp.zeros((40, 128), F32)
        gxr[...] = jnp.zeros((40, 128), F32)
        square[16:128] = jnp.zeros((112, 128), F32)
        for load in loads:
            load.wait()
        square[0:8] = soil[...]
        square[8:9, 0:LEV] = tabs[0]
        turned = square[...].T
        gxl[3:4] = turned[0:1]
        gxr[4:5] = turned[127:128]
        weight[...] = jnp.broadcast_to(turned[0:LEV, 8:9], (LEV, 128))
        square[...] = water[...].T
        gxl[0:3] = square[0:3]
        gxr[5:8] = square[125:128]
        for j in range(3):
            for h in range(2):
                at = j * 16 + h * 8
                main_up[at : at + 8] = water[pl.ds(h * 64 + j, 8, stride=8), :]
                main_down[at : at + 8] = water[pl.ds(h * 64 + 5 + j, 8, stride=8), :]
        main_up[48:56] = soil[...]
        main_down[48:56] = soil[...]

    @pl.when(group == 1)
    def _():
        load_tabs = [
            pltpu.make_async_copy(etab_in, tabs.at[1], sems.at[0]),
            pltpu.make_async_copy(stab_in, tabs.at[2], sems.at[1]),
        ]
        loads = []
        for i, (source, target) in enumerate(
            ((terrain_in, terrain), (cond_in, keff), (mask_in, mask), (head_in, head), (code_in, code_int))
        ):
            parts = []
            for j in range(CHUNKS):
                rows = pl.ds(j * (ROWS // CHUNKS), ROWS // CHUNKS)
                parts.append(pltpu.make_async_copy(source.at[rows], target.at[rows], sems.at[2 + i * CHUNKS + j]))
                parts[-1].start()
            loads.append(parts)

        for load in load_tabs:
            load.start()

        def ready(i):
            for part in loads[i]:
                part.wait()

        ready(1)
        ready(2)
        keff[...] = keff[...] * mask[...].astype(F32)
        ready(4)
        code[...] = code_int[...].astype(F32)
        ready(3)
        ready(0)

        def terrain_at(r, c):
            return terrain[r, c].astype(F32)

        fields = (lambda r, c: keff[r, c], lambda r, c: head[r, c], lambda r, c: code[r, c], terrain_at)
        for f, field in enumerate(fields):
            for t in range(10):
                at = f * 80 + t * 8
                gyu[at : at + 8] = field(slice(0, 8), cut(t))
                gyd[at : at + 8] = field(slice(ROWS - 8, ROWS), cut(t))
        for t in range(10):
            at = 320 + 2 * t
            gyu[at : at + 2] = terrain_at(slice(8, 10), cut(t))
            gyd[at : at + 2] = terrain_at(slice(ROWS - 10, ROWS - 8), cut(t))
        gyu[340:344] = jnp.zeros((4, 128), F32)
        gyd[340:344] = jnp.zeros((4, 128), F32)
        lane = lax.broadcasted_iota(jnp.int32, (ROWS, 128), 1)
        edges = jnp.zeros((ROWS, 128), F32)
        for f, field in enumerate(fields):
            width = 8 if f < 3 else AGG
            first = field(slice(0, ROWS), cut(0))
            last = field(slice(0, ROWS), cut(9))
            first = first if f == 0 else pltpu.roll(first, 8 * f, 1)
            last = pltpu.roll(last, (64 + 8 * f + width) % 128, 1)
            edges = jnp.where((lane >= 8 * f) & (lane < 8 * f + width), first, edges)
            edges = jnp.where((lane >= 64 + 8 * f) & (lane < 64 + 8 * f + width), last, edges)
        square[0:ROWS] = edges
        square[ROWS:128] = jnp.zeros((128 - ROWS, 128), F32)
        square[...] = square[...].T
        gxl[...] = square[0:40]
        gxr[...] = pltpu.roll(square[64:104], 48, 1)
        for load in load_tabs:
            load.wait()


def table_rows(tabs, i):
    return jnp.concatenate([jnp.broadcast_to(tabs[i], (8, NW))] * (128 // NW), axis=1)


def ratio_kernel(tabs, terrain, ew, sw, up_cols, pool_cols, up_rows, pool_rows, found):
    group = lax.axis_index("comp")

    @pl.when(group == 1)
    def _():
        def columns(shape, fine_axis):
            fine = lax.broadcasted_iota(jnp.int32, shape, fine_axis)
            coarse = lax.broadcasted_iota(jnp.int32, shape, 1 - fine_axis)
            first = jnp.where(coarse == 255, WIDE - AGG, jnp.where(coarse <= 128, AGG * coarse, 2 * WIDE))
            return jnp.where((fine >= first) & (fine < first + AGG), 1.0, 0.0).astype(BF)

        up_cols[...] = columns((256, WIDE), 1)
        pool_cols[...] = columns((WIDE, 256), 0)

        def fine_rows(shape, axis):
            at = lax.broadcasted_iota(jnp.int32, shape, axis)
            at = jnp.where(at >= 96, at - 96, at)
            strip = lax.shift_right_logical(at, 3)
            return STRIPS * (at - 8 * strip) + strip

        fine, coarse = fine_rows((192, 64), 0), lax.broadcasted_iota(jnp.int32, (192, 64), 1)
        lower = lax.broadcasted_iota(jnp.int32, (192, 64), 0) >= 96
        mine = jnp.where(coarse >= 32, 1, 0) == jnp.where(lower, 1, 0)
        coarse = lax.rem(coarse, 16)
        own = (fine >= AGG * coarse) & (fine < AGG * coarse + AGG) & (coarse < 8)
        below = (fine >= ROWS) & (fine < ROWS + 8) & (coarse == 8)
        above = (fine >= ROWS + 8) & (coarse == 15)
        up_rows[...] = jnp.where(mine & (own | below | above), 1.0, 0.0).astype(BF)
        fine, coarse = fine_rows((8, 192), 1), lax.broadcasted_iota(jnp.int32, (8, 192), 0)
        pool_rows[...] = jnp.where((fine >= AGG * coarse) & (fine < AGG * coarse + AGG), 1.0, 0.0).astype(BF)

        for i in range(2):
            table = table_rows(tabs, 1 + i)
            for r in range(0, ROWS, 8):
                for t in range(10):
                    found[i * ROWS + r : i * ROWS + r + 8, cut(t)] = jnp.take_along_axis(
                        table, terrain[r : r + 8, cut(t)], axis=1
                    )
        part = dot(both(found[...]), pool_cols[0:COLS, 0:128])
        part = part[0:160] + part[160:320]
        part = jnp.concatenate([part[0:ROWS], part[ROWS:160]], axis=1)
        total = dot(twice(within((8, ROWS), 1)), both(part))
        scale = inverse(total)
        scale = jnp.concatenate([both(scale[:, 0:128]), both(scale[:, 128:256])], axis=0)
        wide = dot(scale, up_cols[0:128, 0:COLS]).astype(BF)
        repeat = twice(within((ROWS, 8), 0))
        ew[...] = found[0:ROWS] * dot(repeat, wide[0:16])
        sw[...] = found[ROWS:160] * dot(repeat, wide[16:32])


def edges_of_grid():
    gy, gx = lax.axis_index("gy"), lax.axis_index("gx")
    has_up = (gy > 0).astype(F32)
    has_down = (gy < lax.axis_size("gy") - 1).astype(F32)
    has_left = (gx > 0).astype(F32)
    has_right = (gx < lax.axis_size("gx") - 1).astype(F32)
    return has_up, has_down, has_left, has_right


def land_kernel(
    water, soil, weight, from_left, from_right, from_up, from_down, coarse, water_out, square, side,
):
    group = lax.axis_index("comp")
    has_up, has_down, has_left, has_right = edges_of_grid()

    @pl.when(group == 0)
    def _():
        pairs = (
            (from_right[0:8], from_left[0:8]),
            (from_down[0:8], from_down[0:8]),
            (from_up[0:8], from_up[0:8]),
        )
        square[8:120] = jnp.zeros((112, 128), F32)
        for i, (right, left) in enumerate(pairs):
            square[0:8] = right
            square[120:128] = left
            side[i] = square[...].T
        lane = lanes()
        for at, (own, down, up) in (
            (0, [pltpu.roll(x[0:8], 5, 0) for x in (from_right, from_down, from_up)]),
            (120, [pltpu.roll(x[0:8], 3, 0) for x in (from_left, from_down, from_up)]),
        ):
            square[at : at + 8] = jnp.where(
                lane < 8, own, jnp.where(lane < 16, pltpu.roll(down, 8, 1), pltpu.roll(up, 16, 1))
            )
        side_soil = square[...].T

        lane2 = lax.broadcasted_iota(jnp.int32, (1, 256), 1)
        col_ok = jnp.where(lane2 < 128, 1.0, jnp.where(lane2 < 192, has_right, has_left))

        def levels(ref, row):
            return jnp.concatenate(
                [ref[pl.ds(h * 64 + row, 8, stride=8), :] for h in range(2)], axis=0
            )

        def side_levels(i, row):
            return jnp.concatenate(
                [side[i, pl.ds(h * 64 + row, 8, stride=8), :] for h in range(2)], axis=0
            )

        field = []
        for j in range(3):
            tile = from_up[8 + j * 16 : 24 + j * 16]
            field.append(jnp.concatenate([tile, side_levels(2, 5 + j)], axis=1) * (col_ok * has_up))
        for j in range(8):
            field.append(jnp.concatenate([levels(water, j), side_levels(0, j)], axis=1) * col_ok)
        for j in range(3):
            tile = from_down[8 + j * 16 : 24 + j * 16]
            field.append(jnp.concatenate([tile, side_levels(1, j)], axis=1) * (col_ok * has_down))

        def sweep(old, first, last):
            new = {}
            for q in range(first, last):
                around = old[q - 1] + old[q + 1] + pltpu.roll(old[q], 1, 1) + pltpu.roll(old[q], 255, 1)
                new[q] = old[q] + diffusion_rate * (around - 4.0 * old[q])
            return new

        once = sweep(field, 1, 13)
        for q in once:
            once[q] = once[q] * (col_ok * (has_up if q < 3 else has_down if q > 10 else 1.0))
        twice = sweep(once, 2, 12)
        for j in range(8):
            water_out[j : j + 1] = twice[3 + j][0:1, 0:128]
        level_weight = jnp.concatenate([weight[...]] * 2, axis=1)
        rain = {q: jnp.sum(level_weight * twice[q] * twice[q], axis=0, keepdims=True) for q in twice}
        blank = jnp.zeros((6, 256), F32)
        rain = jnp.concatenate([rain[3 + j] for j in range(8)] + [rain[11], blank, rain[2]], axis=0)
        moist = jnp.concatenate(
            [
                jnp.concatenate([soil[...], side_soil[0:8]], axis=1),
                jnp.concatenate([from_down[56:57], side_soil[8:9]], axis=1),
                blank,
                jnp.concatenate([from_up[63:64], side_soil[23:24]], axis=1),
            ],
            axis=0,
        )
        coarse[0] = SCALE * rain * moist * moist / (moist * moist + half_point)
        coarse[1] = SCALE * moist


def prepare_kernel(
    keff, head, code, ew, sw, tabs, up_cols, pool_cols, from_left, from_right, from_up, from_down, rows_up, rows_down, after,
    a_e, a_w, a_n, a_s, a_c, m_e, m_w, m_n, m_s, m_c, head_out, ew_out, sw_out,
    square, side, nat, kring, cring, outer, found, near,
):
    group = lax.axis_index("comp")
    has_up, has_down, has_left, has_right = edges_of_grid()

    @pl.when(group == 1)
    def _():
        lane128 = lax.broadcasted_iota(jnp.int32, (40, 128), 1)

        def column(own, down, up):
            return jnp.where(lane128 < 80, own, jnp.where(lane128 < 92, down * has_down, up * has_up))

        square[...] = jnp.zeros((128, 128), F32)
        down, up = from_down[0:40], from_up[0:40]
        square[0:40] = has_right * column(from_right[...], pltpu.roll(down, 80, 1), pltpu.roll(up, 24, 1))
        square[64:104] = has_left * column(
            pltpu.roll(from_left[...], 80, 1), pltpu.roll(down, 32, 1), pltpu.roll(up, 104, 1)
        )
        side[...] = square[...].T
        lane = lax.broadcasted_iota(jnp.int32, (104, 128), 1)

        def columns_of(f, width):
            right = side[0:104] if f == 0 else pltpu.roll(side[0:104], (-8 * f) % 128, 1)
            left = pltpu.roll(side[0:104], (64 - 8 * f - width) % 128, 1)
            return jnp.where(lane < width, right, jnp.where(lane >= 128 - width, left, 0.0))

        def interleave(f):
            for k in range(STRIPS):
                for t in range(TILES):
                    value = nat[t, pl.ds(k, 8, stride=STRIPS), :]
                    if f == 0:
                        kring[k + 1, :, cut(t)] = value
                    elif f == 1:
                        active = kring[k + 1, :, cut(t)] > 0.0
                        head_out[k, :, cut(t)] = jnp.where(active, SCALE * value, 0.0)
                    elif f == 2:
                        cring[k + 1, :, cut(t)] = value
                    elif f == 3:
                        active = kring[k + 1, :, cut(t)] > 0.0
                        ew_out[k, :, cut(t)] = jnp.where(active, value, 0.0)
                    else:
                        sw_out[k, :, cut(t)] = value

        for f, own in enumerate((keff, head, code)):
            for t in range(10):
                at = f * 80 + t * 8
                nat[t, 0:ROWS] = own[:, cut(t)]
                nat[t, ROWS : ROWS + 8] = rows_down[at : at + 8] * has_down
                nat[t, ROWS + 8 : ROWS + 16] = rows_up[at : at + 8] * has_up
            columns = columns_of(f, 8)
            nat[10, 0 : ROWS + 8] = columns[0 : ROWS + 8]
            nat[10, ROWS + 8 : ROWS + 16] = columns[96:104]
            interleave(f)

        corner = columns_of(3, AGG)
        outer[...] = jnp.zeros((32, WIDE), F32)
        for at, rows in ((0, rows_down), (16, rows_up)):
            for t in range(10):
                outer[at : at + 8, cut(t)] = rows[240 + t * 8 : 248 + t * 8]
                outer[at + 8 : at + 10, cut(t)] = rows[320 + t * 2 : 322 + t * 2]
        outer[0:10, cut(10)] = corner[80:90]
        outer[16:24, cut(10)] = corner[96:104]
        outer[24:26, cut(10)] = corner[94:96]
        square[0:ROWS] = corner[0:ROWS]
        for i in range(2):
            table = table_rows(tabs, 1 + i)
            for r in range(0, 32, 8):
                for t in range(TILES):
                    found[i * 32 + r : i * 32 + r + 8, cut(t)] = jnp.take_along_axis(
                        table, outer[r : r + 8, cut(t)].astype(jnp.int32), axis=1
                    )
            for r in range(0, ROWS, 8):
                near[i * ROWS + r : i * ROWS + r + 8] = jnp.take_along_axis(
                    table, square[r : r + 8].astype(jnp.int32), axis=1
                )
        part = dot(both(found[...]), pool_cols[...])
        part = part[0:64] + part[64:128]
        totals = []
        for at in (0, 16, 32, 48):
            totals.append(jnp.sum(part[at : at + 8], axis=0, keepdims=True) + part[at + 8 : at + 9] + part[at + 9 : at + 10])
        scale = inverse(jnp.concatenate(totals + [jnp.zeros((4, 256), F32)], axis=0))
        wide = dot(both(scale), up_cols[...])
        wide = wide[0:8] + wide[8:16]

        col = lax.broadcasted_iota(jnp.int32, (128, 128), 1)
        row = lax.broadcasted_iota(jnp.int32, (128, 128), 0)
        ends = jnp.where(((col == 0) & (row < AGG)) | ((col == 1) & (row >= 128 - AGG)), 1.0, 0.0).astype(BF)
        part = dot(both(near[...]), ends)
        part = part[0:160] + part[160:320]
        part = jnp.concatenate([part[0:ROWS], part[ROWS:160]], axis=1)
        scale = inverse(dot(twice(within((8, ROWS), 1)), both(part)))
        scale = dot(twice(within((ROWS, 8), 0)), both(scale))
        first = lax.broadcasted_iota(jnp.int32, (ROWS, 128), 1) < AGG
        for i, own in enumerate((ew, sw)):
            for t in range(TILES):
                nat[t, ROWS : ROWS + 8] = found[32 * i : 32 * i + 8, cut(t)] * wide[2 * i : 2 * i + 1, cut(t)]
                nat[t, ROWS + 8 : ROWS + 16] = (
                    found[32 * i + 16 : 32 * i + 24, cut(t)] * wide[2 * i + 1 : 2 * i + 2, cut(t)]
                )
            at = 128 * i
            nat[10, 0:ROWS] = near[i * ROWS : (i + 1) * ROWS] * jnp.where(
                first, scale[:, at : at + 1], scale[:, at + 1 : at + 2]
            )
            for t in range(10):
                nat[t, 0:ROWS] = own[:, cut(t)]
            interleave(3 + i)
        for ring in (kring, cring):
            for t in range(TILES):
                ring[0, :, cut(t)] = pltpu.roll(ring[STRIPS, :, cut(t)], 1, 0)
                ring[STRIPS + 1, :, cut(t)] = pltpu.roll(ring[1, :, cut(t)], 7, 0)

        lane = lanes()
        for k in range(STRIPS):
            here = [kring[k + 1, :, cut(t)] for t in range(TILES)]
            codes = [cring[k + 1, :, cut(t)] for t in range(TILES)]
            west, east = beside(here, lane)

            def drains(cond, codes, number):
                return jnp.where((cond > 0.0) & (codes == number), drainage_rate / SCALE, 0.0)

            to_east, _ = beside([drains(here[t], codes[t], 3.0) for t in range(TILES)], lane)
            _, to_west = beside([drains(here[t], codes[t], 2.0) for t in range(TILES)], lane)
            for t in range(TILES):
                north, south = kring[k, :, cut(t)], kring[k + 2, :, cut(t)]
                n, s = jnp.sqrt(here[t] * north), jnp.sqrt(here[t] * south)
                w, e = jnp.sqrt(here[t] * west[t]), jnp.sqrt(here[t] * east[t])
                a_n[k, :, cut(t)] = n
                a_s[k, :, cut(t)] = s
                a_w[k, :, cut(t)] = w
                a_e[k, :, cut(t)] = e
                a_c[k, :, cut(t)] = 1.0 - ((n + s) + (w + e))
                m_n[k, :, cut(t)] = drains(north, cring[k, :, cut(t)], 1.0)
                m_s[k, :, cut(t)] = drains(south, cring[k + 2, :, cut(t)], 0.0)
                m_w[k, :, cut(t)] = to_east[t]
                m_e[k, :, cut(t)] = to_west[t]
                m_c[k, :, cut(t)] = jnp.where(here[t] > 0.0, drainage_rate / SCALE, 0.0)


def route_kernel(
    coarse, a_e, a_w, a_n, a_s, a_c, m_e, m_w, m_n, m_s, m_c, head, ew, sw, up_cols, up_rows, pool_cols, pool_rows,
    ponded_out, stored_out, pond_a, pond_b, store, square_a, square_b,
):
    group = lax.axis_index("comp")

    @pl.when(group == 1)
    def _():
        pieces = jnp.concatenate([*split(coarse[0]), *split(coarse[1])], axis=0)
        fields = dot(up_rows[...], dot(pieces, up_cols[...]).astype(BF))
        excess, moist = fields[0:96], fields[96:192]
        pond_a[1 : STRIPS + 1] = head[...] + ew[...] * excess.reshape(STRIPS, 8, WIDE)
        store[...] = sw[...] * moist.reshape(STRIPS, 8, WIDE)
        square_a[1 : STRIPS + 1] = store[...] * store[...]

        def close(ring):
            for t in range(TILES):
                ring[0, :, cut(t)] = pltpu.roll(ring[STRIPS, :, cut(t)], 1, 0)
                ring[STRIPS + 1, :, cut(t)] = pltpu.roll(ring[1, :, cut(t)], 7, 0)

        close(pond_a)
        close(square_a)

        def substep(pond, square, new_pond, new_square):
            lane = lanes()
            first, last = lane == 0, lane == 127
            for k in range(STRIPS):
                p, q = pond[k + 1, :, cut(0)], square[k + 1, :, cut(0)]
                p_left, q_left = pltpu.roll(p, 127, 1), pltpu.roll(q, 127, 1)
                p_before = pltpu.roll(pond[k + 1, :, cut(TILES - 1)], 1, 1)
                q_before = pltpu.roll(square[k + 1, :, cut(TILES - 1)], 1, 1)
                for t in range(TILES):
                    c, after = cut(t), cut((t + 1) % TILES)
                    p_next, q_next = pond[k + 1, :, after], square[k + 1, :, after]
                    p_right, q_right = pltpu.roll(p, 1, 1), pltpu.roll(q, 1, 1)
                    p_next_left, q_next_left = pltpu.roll(p_next, 127, 1), pltpu.roll(q_next, 127, 1)
                    p_w, p_e = jnp.where(first, p_before, p_right), jnp.where(last, p_next_left, p_left)
                    q_w, q_e = jnp.where(first, q_before, q_right), jnp.where(last, q_next_left, q_left)
                    s = store[k, :, c]
                    soaked = p * pltpu.reciprocal(SCALE + s, approx=True)
                    flow = a_n[k, :, c] * pond[k, :, c] + a_s[k, :, c] * pond[k + 2, :, c]
                    flow = flow + (a_w[k, :, c] * p_w + a_e[k, :, c] * p_e)
                    new_pond[k + 1, :, c] = a_c[k, :, c] * p + flow - soaked
                    inflow = m_n[k, :, c] * square[k, :, c] + m_s[k, :, c] * square[k + 2, :, c]
                    inflow = inflow + (m_w[k, :, c] * q_w + m_e[k, :, c] * q_e)
                    s = (s + soaked) + (inflow - m_c[k, :, c] * q)
                    store[k, :, c] = s
                    new_square[k + 1, :, c] = s * s
                    p, q, p_left, q_left = p_next, q_next, p_next_left, q_next_left
                    p_before, q_before = p_right, q_right
            close(new_pond)
            close(new_square)

        def two(i, carry):
            substep(pond_a, square_a, pond_b, square_b)
            substep(pond_b, square_b, pond_a, square_a)
            return carry

        lax.fori_loop(0, NSUB // 2, two, 0)
        pieces = []
        for last in (pond_a[1 : STRIPS + 1], store[...]):
            pieces.extend(split(last.reshape(STRIPS * 8, WIDE)))
        part = dot(jnp.concatenate(pieces, axis=0), pool_cols[:, 0:128])
        part = jnp.concatenate([part[0:96] + part[96:192], part[192:288] + part[288:384]], axis=1)
        mean = dot(pool_rows[...], both(part)) * (1.0 / (SCALE * AGG * AGG))
        ponded_out[...] = mean[:, 0:128]
        stored_out[...] = mean[:, 128:256]


def moved(array, mesh_shape, target):
    groups, ys, xs = mesh_shape
    pairs = []
    for g in range(groups):
        for y in range(ys):
            for x in range(xs):
                a, b, c = target(g, y, x)
                pairs.append(((g * ys + y) * xs + x, ((a % groups) * ys + b % ys) * xs + c % xs))
    return lax.ppermute(array, ("comp", "gy", "gx"), pairs)


def f32(*shape):
    return jax.ShapeDtypeStruct(shape, F32)


def per_device(
    column_water,
    land_soil,
    level_weight,
    excess_weight,
    soil_weight,
    terrain_class,
    surface_head,
    conductivity,
    active_mask,
    flow_code,
):
    shape = tuple(lax.axis_size(axis) for axis in ("comp", "gy", "gx"))
    group = lax.axis_index("comp")
    params = pltpu.CompilerParams(vmem_limit_bytes=32 * 1024 * 1024)
    arguments = (
        column_water[0].reshape(128, 128), land_soil[0], level_weight[None], excess_weight[None], soil_weight[None],
        terrain_class, surface_head[0], conductivity[0], active_mask[0], flow_code[0],
    )
    hbm = pl.BlockSpec(memory_space=pltpu.HBM)
    fine = f32(ROWS, COLS)
    fine_int = pltpu.VMEM((ROWS, COLS), jnp.int32)
    gxl, gxr, main_up, main_down, gyu, gyd, water, soil, weight, tabs, terrain, keff, head, code = pl.pallas_call(
        pack_kernel,
        in_specs=[hbm] * 10,
        out_shape=[f32(40, 128)] * 2
        + [f32(56, 128)] * 2
        + [f32(344, 128)] * 2
        + [f32(128, 128), f32(8, 128), f32(LEV, 128), f32(3, 1, NW)]
        + [jax.ShapeDtypeStruct((ROWS, COLS), jnp.int32)]
        + [fine] * 3,
        scratch_shapes=[
            pltpu.VMEM((128, 128), F32),
            fine_int,
            fine_int,
            pltpu.SemaphoreType.DMA((2 + 5 * CHUNKS,)),
        ],
        compiler_params=params,
        name="pack",
    )(*(pltpu.with_memory_space_constraint(array, pltpu.HBM) for array in arguments))
    ew, sw, up_cols, pool_cols, up_rows, pool_rows = pl.pallas_call(
        ratio_kernel,
        out_shape=[fine] * 2
        + [jax.ShapeDtypeStruct(dims, BF) for dims in ((256, WIDE), (WIDE, 256), (192, 64), (8, 192))],
        scratch_shapes=[pltpu.VMEM((2 * ROWS, COLS), F32)],
        compiler_params=params,
        name="ratio",
    )(tabs, terrain)
    from_left = moved(gxr, shape, lambda g, y, x: (g, y, x + 1))
    from_right = moved(gxl, shape, lambda g, y, x: (g, y, x - 1))
    rows_up = moved(gyd, shape, lambda g, y, x: (g, y + 1, x) if g else (g, y, x ^ 1))
    rows_down = moved(gyu, shape, lambda g, y, x: (g, y - 1, x) if g else (g, y, x ^ 1))
    row = lax.broadcasted_iota(jnp.int32, (8, 128), 0)
    halo = jnp.where(row < 4, from_right[:8], from_left[:8])
    land_up = moved(
        jnp.concatenate([halo, main_down]), shape, lambda g, y, x: (g, y, x ^ 1) if g else (g, y + 1, x)
    )
    land_down = moved(
        jnp.concatenate([halo, main_up]), shape, lambda g, y, x: (g, y, x ^ 1) if g else (g, y - 1, x)
    )
    lane = lax.broadcasted_iota(jnp.int32, (40, 128), 1)
    route_up = moved(
        jnp.concatenate([jnp.where(lane < 100, from_right, from_left), jnp.zeros((32, 128), F32)]), shape, lambda g, y, x: (g, y + 1, x) if g else (g, y, x ^ 1)
    )
    route_down = moved(
        jnp.concatenate([jnp.where(lane < 40, from_right, from_left), jnp.zeros((32, 128), F32)]), shape, lambda g, y, x: (g, y - 1, x) if g else (g, y, x ^ 1)
    )
    coarse, water_top = pl.pallas_call(
        land_kernel,
        out_shape=[f32(2, 16, 256), f32(8, 128)],
        scratch_shapes=[pltpu.VMEM((128, 128), F32), pltpu.VMEM((3, 128, 128), F32)],
        compiler_params=params,
        name="land",
    )(water, soil, weight, from_left, from_right, land_up, land_down)
    arrived = moved(coarse, shape, lambda g, y, x: (1 - g, y, x))
    strips = f32(STRIPS, 8, WIDE)
    ring = pltpu.VMEM((STRIPS + 2, 8, WIDE), F32)
    prepared = pl.pallas_call(
        prepare_kernel,
        out_shape=[strips] * 13,
        scratch_shapes=[
            pltpu.VMEM((128, 128), F32),
            pltpu.VMEM((128, 128), F32),
            pltpu.VMEM((TILES, 96, 128), F32),
            ring,
            ring,
            pltpu.VMEM((32, WIDE), F32),
            pltpu.VMEM((64, WIDE), F32),
            pltpu.VMEM((2 * ROWS, 128), F32),
        ],
        compiler_params=params,
        name="prepare",
    )(
        keff, head, code, ew, sw, tabs, up_cols, pool_cols, from_left, from_right, route_up, route_down,
        rows_up, rows_down, water_top,
    )
    ring = pltpu.VMEM((STRIPS + 2, 8, WIDE), F32)
    ponded, stored = pl.pallas_call(
        route_kernel,
        out_shape=[f32(8, 128), f32(8, 128)],
        scratch_shapes=[ring] * 2 + [pltpu.VMEM((STRIPS, 8, WIDE), F32)] + [ring] * 2,
        compiler_params=params,
        name="route",
    )(arrived, *prepared, up_cols, up_rows, pool_cols, pool_rows)
    returned = moved(stored, shape, lambda g, y, x: (1 - g, y, x))
    land_out = returned / (1.0 + evaporation_scale * water_top * water_top)
    return jnp.where(group == 0, land_out, ponded)[None]


def solution(mesh):
    in_specs = (
        P("comp", None, "gy", "gx"),
        P("comp", "gy", "gx"),
        P(),
        P(),
        P(),
        P("gy", "gx"),
        P("comp", "gy", "gx"),
        P("comp", "gy", "gx"),
        P("comp", "gy", "gx"),
        P("comp", "gy", "gx"),
    )
    out_specs = P("comp", "gy", "gx")
    return jax.shard_map(
        per_device, mesh=mesh, in_specs=in_specs, out_specs=out_specs, check_vma=False
    )
```

```python
import jax
import jax.numpy as jnp
from jax import lax
from jax.experimental import pallas as pl
from jax.experimental.pallas import tpu as pltpu
from jax.sharding import PartitionSpec as P

AGG = 10
NSUB = 8
LEV = 16
ROWS = 80
COLS = 1280
HALO = 8
STRIPS = 12
TILES = 11
WIDE = TILES * 128
CHUNKS = 1
NW = 16
BF = jnp.bfloat16
F32 = jnp.float32

diffusion_rate = 0.2
infiltration_rate = 0.05
drainage_rate = 0.1
half_point = 0.1
evaporation_scale = 0.5
SCALE = 1.0 / infiltration_rate


def split(x):
    high = x.astype(BF)
    return high, (x - high.astype(F32)).astype(BF)


def dot(a, b):
    return jnp.dot(a, b, preferred_element_type=F32)


def both(x):
    return jnp.concatenate(split(x), axis=0)


def inverse(total):
    return float(AGG * AGG) / jnp.where(total > 0.0, total, 1.0)


def twice(x):
    return jnp.concatenate([x, x], axis=1)


def lanes():
    return lax.broadcasted_iota(jnp.int32, (8, 128), 1)


def beside(tiles, lane):
    right = [pltpu.roll(x, 1, 1) for x in tiles]
    left = [pltpu.roll(x, 127, 1) for x in tiles]
    n = len(tiles)
    west = [jnp.where(lane == 0, right[t - 1], right[t]) for t in range(n)]
    east = [jnp.where(lane == 127, left[(t + 1) % n], left[t]) for t in range(n)]
    return west, east


def cut(t):
    return slice(t * 128, (t + 1) * 128)


def within(shape, fine_axis):
    fine = lax.broadcasted_iota(jnp.int32, shape, fine_axis)
    first = AGG * lax.broadcasted_iota(jnp.int32, shape, 1 - fine_axis)
    return jnp.where((fine >= first) & (fine < first + AGG), 1.0, 0.0).astype(BF)


def pack_kernel(
    water_in, soil_in, weight_in, etab_in, stab_in, terrain_in, head_in, cond_in, mask_in, code_in,
    gxl, gxr, main_up, main_down, gyu, gyd, extra_up, extra_down, water, soil, weight, tabs, terrain, keff, head, code,
    square, mask, code_int, sems,
):
    group = lax.axis_index("comp")

    @pl.when(group == 0)
    def _():
        loads = [
            pltpu.make_async_copy(water_in, water, sems.at[0]),
            pltpu.make_async_copy(soil_in, soil, sems.at[1]),
            pltpu.make_async_copy(weight_in, tabs.at[0], sems.at[2]),
        ]
        for load in loads:
            load.start()
        gxl[...] = jnp.zeros((40, 128), F32)
        gxr[...] = jnp.zeros((40, 128), F32)
        square[16:128] = jnp.zeros((112, 128), F32)
        for load in loads:
            load.wait()
        square[0:8] = soil[...]
        square[8:9, 0:LEV] = tabs[0]
        turned = square[...].T
        gxl[3:4] = turned[0:1]
        gxr[4:5] = turned[127:128]
        weight[...] = jnp.broadcast_to(turned[0:LEV, 8:9], (LEV, 128))
        square[...] = water[...].T
        gxl[0:3] = square[0:3]
        gxr[5:8] = square[125:128]
        for j in range(3):
            for h in range(2):
                at = j * 16 + h * 8
                main_up[at : at + 8] = water[pl.ds(h * 64 + j, 8, stride=8), :]
                main_down[at : at + 8] = water[pl.ds(h * 64 + 5 + j, 8, stride=8), :]
        main_up[48:56] = soil[...]
        main_down[48:56] = soil[...]

    @pl.when(group == 1)
    def _():
        load_tabs = [
            pltpu.make_async_copy(etab_in, tabs.at[1], sems.at[0]),
            pltpu.make_async_copy(stab_in, tabs.at[2], sems.at[1]),
        ]
        loads = []
        for i, (source, target) in enumerate(
            ((terrain_in, terrain), (cond_in, keff), (mask_in, mask), (head_in, head), (code_in, code_int))
        ):
            parts = []
            for j in range(CHUNKS):
                rows = pl.ds(j * (ROWS // CHUNKS), ROWS // CHUNKS)
                parts.append(pltpu.make_async_copy(source.at[rows], target.at[rows], sems.at[2 + i * CHUNKS + j]))
                parts[-1].start()
            loads.append(parts)

        for load in load_tabs:
            load.start()

        def ready(i):
            for part in loads[i]:
                part.wait()

        ready(1)
        ready(2)
        keff[...] = keff[...] * mask[...].astype(F32)
        ready(4)
        code[...] = code_int[...].astype(F32)
        ready(3)
        ready(0)

        def terrain_at(r, c):
            return terrain[r, c].astype(F32)

        fields = (lambda r, c: keff[r, c], lambda r, c: head[r, c], lambda r, c: code[r, c], terrain_at)
        for f, field in enumerate(fields):
            for t in range(10):
                at = f * 80 + t * 8
                gyu[at : at + 8] = field(slice(0, 8), cut(t))
                gyd[at : at + 8] = field(slice(ROWS - 8, ROWS), cut(t))
        for t in range(10):
            extra_up[2 * t : 2 * t + 2] = terrain_at(slice(8, 10), cut(t))
            extra_down[2 * t : 2 * t + 2] = terrain_at(slice(ROWS - 10, ROWS - 8), cut(t))
        extra_up[20:40] = jnp.zeros((20, 128), F32)
        extra_down[20:40] = jnp.zeros((20, 128), F32)
        lane = lax.broadcasted_iota(jnp.int32, (ROWS, 128), 1)
        edges = jnp.zeros((ROWS, 128), F32)
        for f, field in enumerate(fields):
            width = 8 if f < 3 else AGG
            first = field(slice(0, ROWS), cut(0))
            last = field(slice(0, ROWS), cut(9))
            first = first if f == 0 else pltpu.roll(first, 8 * f, 1)
            last = pltpu.roll(last, (64 + 8 * f + width) % 128, 1)
            edges = jnp.where((lane >= 8 * f) & (lane < 8 * f + width), first, edges)
            edges = jnp.where((lane >= 64 + 8 * f) & (lane < 64 + 8 * f + width), last, edges)
        square[0:ROWS] = edges
        square[ROWS:128] = jnp.zeros((128 - ROWS, 128), F32)
        square[...] = square[...].T
        gxl[...] = square[0:40]
        gxr[...] = pltpu.roll(square[64:104], 48, 1)
        for load in load_tabs:
            load.wait()


def table_rows(tabs, i):
    return jnp.concatenate([jnp.broadcast_to(tabs[i], (8, NW))] * (128 // NW), axis=1)


def ratio_kernel(tabs, terrain, ew, sw, up_cols, pool_cols, up_rows, pool_rows, found):
    group = lax.axis_index("comp")

    @pl.when(group == 1)
    def _():
        def columns(shape, fine_axis):
            fine = lax.broadcasted_iota(jnp.int32, shape, fine_axis)
            coarse = lax.broadcasted_iota(jnp.int32, shape, 1 - fine_axis)
            first = jnp.where(coarse == 255, WIDE - AGG, jnp.where(coarse <= 128, AGG * coarse, 2 * WIDE))
            return jnp.where((fine >= first) & (fine < first + AGG), 1.0, 0.0).astype(BF)

        up_cols[...] = columns((256, WIDE), 1)
        pool_cols[...] = columns((WIDE, 256), 0)

        def fine_rows(shape, axis):
            at = lax.broadcasted_iota(jnp.int32, shape, axis)
            at = jnp.where(at >= 96, at - 96, at)
            strip = lax.shift_right_logical(at, 3)
            return STRIPS * (at - 8 * strip) + strip

        fine, coarse = fine_rows((192, 64), 0), lax.broadcasted_iota(jnp.int32, (192, 64), 1)
        lower = lax.broadcasted_iota(jnp.int32, (192, 64), 0) >= 96
        mine = jnp.where(coarse >= 32, 1, 0) == jnp.where(lower, 1, 0)
        coarse = lax.rem(coarse, 16)
        own = (fine >= AGG * coarse) & (fine < AGG * coarse + AGG) & (coarse < 8)
        below = (fine >= ROWS) & (fine < ROWS + 8) & (coarse == 8)
        above = (fine >= ROWS + 8) & (coarse == 15)
        up_rows[...] = jnp.where(mine & (own | below | above), 1.0, 0.0).astype(BF)
        fine, coarse = fine_rows((8, 192), 1), lax.broadcasted_iota(jnp.int32, (8, 192), 0)
        pool_rows[...] = jnp.where((fine >= AGG * coarse) & (fine < AGG * coarse + AGG), 1.0, 0.0).astype(BF)

        for i in range(2):
            table = table_rows(tabs, 1 + i)
            for r in range(0, ROWS, 8):
                for t in range(10):
                    found[i * ROWS + r : i * ROWS + r + 8, cut(t)] = jnp.take_along_axis(
                        table, terrain[r : r + 8, cut(t)], axis=1
                    )
        part = dot(both(found[...]), pool_cols[0:COLS, 0:128])
        part = part[0:160] + part[160:320]
        part = jnp.concatenate([part[0:ROWS], part[ROWS:160]], axis=1)
        total = dot(twice(within((8, ROWS), 1)), both(part))
        scale = inverse(total)
        scale = jnp.concatenate([both(scale[:, 0:128]), both(scale[:, 128:256])], axis=0)
        wide = dot(scale, up_cols[0:128, 0:COLS]).astype(BF)
        repeat = twice(within((ROWS, 8), 0))
        ew[...] = found[0:ROWS] * dot(repeat, wide[0:16])
        sw[...] = found[ROWS:160] * dot(repeat, wide[16:32])


def edges_of_grid():
    gy, gx = lax.axis_index("gy"), lax.axis_index("gx")
    has_up = (gy > 0).astype(F32)
    has_down = (gy < lax.axis_size("gy") - 1).astype(F32)
    has_left = (gx > 0).astype(F32)
    has_right = (gx < lax.axis_size("gx") - 1).astype(F32)
    return has_up, has_down, has_left, has_right


def land_kernel(
    water, soil, weight, from_left, from_right, from_up, from_down, coarse, water_out, square, side,
):
    group = lax.axis_index("comp")
    has_up, has_down, has_left, has_right = edges_of_grid()

    @pl.when(group == 0)
    def _():
        pairs = (
            (from_right[0:8], from_left[0:8]),
            (from_down[0:8], from_down[0:8]),
            (from_up[0:8], from_up[0:8]),
        )
        square[8:120] = jnp.zeros((112, 128), F32)
        for i, (right, left) in enumerate(pairs):
            square[0:8] = right
            square[120:128] = left
            side[i] = square[...].T
        lane = lanes()
        for at, (own, down, up) in (
            (0, [pltpu.roll(x[0:8], 5, 0) for x in (from_right, from_down, from_up)]),
            (120, [pltpu.roll(x[0:8], 3, 0) for x in (from_left, from_down, from_up)]),
        ):
            square[at : at + 8] = jnp.where(
                lane < 8, own, jnp.where(lane < 16, pltpu.roll(down, 8, 1), pltpu.roll(up, 16, 1))
            )
        side_soil = square[...].T

        lane2 = lax.broadcasted_iota(jnp.int32, (1, 256), 1)
        col_ok = jnp.where(lane2 < 128, 1.0, jnp.where(lane2 < 192, has_right, has_left))

        def levels(ref, row):
            return jnp.concatenate(
                [ref[pl.ds(h * 64 + row, 8, stride=8), :] for h in range(2)], axis=0
            )

        def side_levels(i, row):
            return jnp.concatenate(
                [side[i, pl.ds(h * 64 + row, 8, stride=8), :] for h in range(2)], axis=0
            )

        field = []
        for j in range(3):
            tile = from_up[8 + j * 16 : 24 + j * 16]
            field.append(jnp.concatenate([tile, side_levels(2, 5 + j)], axis=1) * (col_ok * has_up))
        for j in range(8):
            field.append(jnp.concatenate([levels(water, j), side_levels(0, j)], axis=1) * col_ok)
        for j in range(3):
            tile = from_down[8 + j * 16 : 24 + j * 16]
            field.append(jnp.concatenate([tile, side_levels(1, j)], axis=1) * (col_ok * has_down))

        def sweep(old, first, last):
            new = {}
            for q in range(first, last):
                around = old[q - 1] + old[q + 1] + pltpu.roll(old[q], 1, 1) + pltpu.roll(old[q], 255, 1)
                new[q] = old[q] + diffusion_rate * (around - 4.0 * old[q])
            return new

        once = sweep(field, 1, 13)
        for q in once:
            once[q] = once[q] * (col_ok * (has_up if q < 3 else has_down if q > 10 else 1.0))
        twice = sweep(once, 2, 12)
        for j in range(8):
            water_out[j : j + 1] = twice[3 + j][0:1, 0:128]
        level_weight = jnp.concatenate([weight[...]] * 2, axis=1)
        rain = {q: jnp.sum(level_weight * twice[q] * twice[q], axis=0, keepdims=True) for q in twice}
        blank = jnp.zeros((6, 256), F32)
        rain = jnp.concatenate([rain[3 + j] for j in range(8)] + [rain[11], blank, rain[2]], axis=0)
        moist = jnp.concatenate(
            [
                jnp.concatenate([soil[...], side_soil[0:8]], axis=1),
                jnp.concatenate([from_down[56:57], side_soil[8:9]], axis=1),
                blank,
                jnp.concatenate([from_up[63:64], side_soil[23:24]], axis=1),
            ],
            axis=0,
        )
        coarse[0] = SCALE * rain * moist * moist / (moist * moist + half_point)
        coarse[1] = SCALE * moist


def prepare_kernel(
    keff, head, code, ew, sw, tabs, up_cols, pool_cols, from_left, from_right, from_up, from_down, rows_up, rows_down, after,
    a_e, a_w, a_n, a_s, a_c, m_e, m_w, m_n, m_s, m_c, head_out, ew_out, sw_out,
    square, side, nat, kring, cring, outer, found, near,
):
    group = lax.axis_index("comp")
    has_up, has_down, has_left, has_right = edges_of_grid()

    @pl.when(group == 1)
    def _():
        lane128 = lax.broadcasted_iota(jnp.int32, (40, 128), 1)

        def column(own, down, up):
            return jnp.where(lane128 < 80, own, jnp.where(lane128 < 92, down * has_down, up * has_up))

        square[...] = jnp.zeros((128, 128), F32)
        down, up = from_down[0:40], from_up[0:40]
        square[0:40] = has_right * column(from_right[...], pltpu.roll(down, 80, 1), pltpu.roll(up, 24, 1))
        square[64:104] = has_left * column(
            pltpu.roll(from_left[...], 80, 1), pltpu.roll(down, 32, 1), pltpu.roll(up, 104, 1)
        )
        side[...] = square[...].T
        lane = lax.broadcasted_iota(jnp.int32, (104, 128), 1)

        def columns_of(f, width):
            right = side[0:104] if f == 0 else pltpu.roll(side[0:104], (-8 * f) % 128, 1)
            left = pltpu.roll(side[0:104], (64 - 8 * f - width) % 128, 1)
            return jnp.where(lane < width, right, jnp.where(lane >= 128 - width, left, 0.0))

        def interleave(f):
            for k in range(STRIPS):
                for t in range(TILES):
                    value = nat[t, pl.ds(k, 8, stride=STRIPS), :]
                    if f == 0:
                        kring[k + 1, :, cut(t)] = value
                    elif f == 1:
                        active = kring[k + 1, :, cut(t)] > 0.0
                        head_out[k, :, cut(t)] = jnp.where(active, SCALE * value, 0.0)
                    elif f == 2:
                        cring[k + 1, :, cut(t)] = value
                    elif f == 3:
                        active = kring[k + 1, :, cut(t)] > 0.0
                        ew_out[k, :, cut(t)] = jnp.where(active, value, 0.0)
                    else:
                        sw_out[k, :, cut(t)] = value

        for f, own in enumerate((keff, head, code)):
            for t in range(10):
                at = f * 80 + t * 8
                nat[t, 0:ROWS] = own[:, cut(t)]
                nat[t, ROWS : ROWS + 8] = rows_down[at : at + 8] * has_down
                nat[t, ROWS + 8 : ROWS + 16] = rows_up[at : at + 8] * has_up
            columns = columns_of(f, 8)
            nat[10, 0 : ROWS + 8] = columns[0 : ROWS + 8]
            nat[10, ROWS + 8 : ROWS + 16] = columns[96:104]
            interleave(f)

        corner = columns_of(3, AGG)
        outer[...] = jnp.zeros((32, WIDE), F32)
        for at, rows, extra in ((0, rows_down, from_down), (16, rows_up, from_up)):
            for t in range(10):
                outer[at : at + 8, cut(t)] = rows[240 + t * 8 : 248 + t * 8]
                outer[at + 8 : at + 10, cut(t)] = extra[40 + t * 2 : 42 + t * 2]
        outer[0:10, cut(10)] = corner[80:90]
        outer[16:24, cut(10)] = corner[96:104]
        outer[24:26, cut(10)] = corner[94:96]
        square[0:ROWS] = corner[0:ROWS]
        for i in range(2):
            table = table_rows(tabs, 1 + i)
            for r in range(0, 32, 8):
                for t in range(TILES):
                    found[i * 32 + r : i * 32 + r + 8, cut(t)] = jnp.take_along_axis(
                        table, outer[r : r + 8, cut(t)].astype(jnp.int32), axis=1
                    )
            for r in range(0, ROWS, 8):
                near[i * ROWS + r : i * ROWS + r + 8] = jnp.take_along_axis(
                    table, square[r : r + 8].astype(jnp.int32), axis=1
                )
        part = dot(both(found[...]), pool_cols[...])
        part = part[0:64] + part[64:128]
        totals = []
        for at in (0, 16, 32, 48):
            totals.append(jnp.sum(part[at : at + 8], axis=0, keepdims=True) + part[at + 8 : at + 9] + part[at + 9 : at + 10])
        scale = inverse(jnp.concatenate(totals + [jnp.zeros((4, 256), F32)], axis=0))
        wide = dot(both(scale), up_cols[...])
        wide = wide[0:8] + wide[8:16]

        col = lax.broadcasted_iota(jnp.int32, (128, 128), 1)
        row = lax.broadcasted_iota(jnp.int32, (128, 128), 0)
        ends = jnp.where(((col == 0) & (row < AGG)) | ((col == 1) & (row >= 128 - AGG)), 1.0, 0.0).astype(BF)
        part = dot(both(near[...]), ends)
        part = part[0:160] + part[160:320]
        part = jnp.concatenate([part[0:ROWS], part[ROWS:160]], axis=1)
        scale = inverse(dot(twice(within((8, ROWS), 1)), both(part)))
        scale = dot(twice(within((ROWS, 8), 0)), both(scale))
        first = lax.broadcasted_iota(jnp.int32, (ROWS, 128), 1) < AGG
        for i, own in enumerate((ew, sw)):
            for t in range(TILES):
                nat[t, ROWS : ROWS + 8] = found[32 * i : 32 * i + 8, cut(t)] * wide[2 * i : 2 * i + 1, cut(t)]
                nat[t, ROWS + 8 : ROWS + 16] = (
                    found[32 * i + 16 : 32 * i + 24, cut(t)] * wide[2 * i + 1 : 2 * i + 2, cut(t)]
                )
            at = 128 * i
            nat[10, 0:ROWS] = near[i * ROWS : (i + 1) * ROWS] * jnp.where(
                first, scale[:, at : at + 1], scale[:, at + 1 : at + 2]
            )
            for t in range(10):
                nat[t, 0:ROWS] = own[:, cut(t)]
            interleave(3 + i)
        for ring in (kring, cring):
            for t in range(TILES):
                ring[0, :, cut(t)] = pltpu.roll(ring[STRIPS, :, cut(t)], 1, 0)
                ring[STRIPS + 1, :, cut(t)] = pltpu.roll(ring[1, :, cut(t)], 7, 0)

        lane = lanes()
        for k in range(STRIPS):
            here = [kring[k + 1, :, cut(t)] for t in range(TILES)]
            codes = [cring[k + 1, :, cut(t)] for t in range(TILES)]
            west, east = beside(here, lane)

            def drains(cond, codes, number):
                return jnp.where((cond > 0.0) & (codes == number), drainage_rate / SCALE, 0.0)

            to_east, _ = beside([drains(here[t], codes[t], 3.0) for t in range(TILES)], lane)
            _, to_west = beside([drains(here[t], codes[t], 2.0) for t in range(TILES)], lane)
            for t in range(TILES):
                north, south = kring[k, :, cut(t)], kring[k + 2, :, cut(t)]
                n, s = jnp.sqrt(here[t] * north), jnp.sqrt(here[t] * south)
                w, e = jnp.sqrt(here[t] * west[t]), jnp.sqrt(here[t] * east[t])
                a_n[k, :, cut(t)] = n
                a_s[k, :, cut(t)] = s
                a_w[k, :, cut(t)] = w
                a_e[k, :, cut(t)] = e
                a_c[k, :, cut(t)] = 1.0 - ((n + s) + (w + e))
                m_n[k, :, cut(t)] = drains(north, cring[k, :, cut(t)], 1.0)
                m_s[k, :, cut(t)] = drains(south, cring[k + 2, :, cut(t)], 0.0)
                m_w[k, :, cut(t)] = to_east[t]
                m_e[k, :, cut(t)] = to_west[t]
                m_c[k, :, cut(t)] = jnp.where(here[t] > 0.0, drainage_rate / SCALE, 0.0)


def route_kernel(
    coarse, a_e, a_w, a_n, a_s, a_c, m_e, m_w, m_n, m_s, m_c, head, ew, sw, up_cols, up_rows, pool_cols, pool_rows,
    ponded_out, stored_out, pond_a, pond_b, store, square_a, square_b,
):
    group = lax.axis_index("comp")

    @pl.when(group == 1)
    def _():
        pieces = jnp.concatenate([*split(coarse[0]), *split(coarse[1])], axis=0)
        fields = dot(up_rows[...], dot(pieces, up_cols[...]).astype(BF))
        excess, moist = fields[0:96], fields[96:192]
        pond_a[1 : STRIPS + 1] = head[...] + ew[...] * excess.reshape(STRIPS, 8, WIDE)
        store[...] = sw[...] * moist.reshape(STRIPS, 8, WIDE)
        square_a[1 : STRIPS + 1] = store[...] * store[...]

        def close(ring):
            for t in range(TILES):
                ring[0, :, cut(t)] = pltpu.roll(ring[STRIPS, :, cut(t)], 1, 0)
                ring[STRIPS + 1, :, cut(t)] = pltpu.roll(ring[1, :, cut(t)], 7, 0)

        close(pond_a)
        close(square_a)

        def substep(pond, square, new_pond, new_square):
            lane = lanes()
            first, last = lane == 0, lane == 127
            for k in range(STRIPS):
                p, q = pond[k + 1, :, cut(0)], square[k + 1, :, cut(0)]
                p_left, q_left = pltpu.roll(p, 127, 1), pltpu.roll(q, 127, 1)
                p_before = pltpu.roll(pond[k + 1, :, cut(TILES - 1)], 1, 1)
                q_before = pltpu.roll(square[k + 1, :, cut(TILES - 1)], 1, 1)
                for t in range(TILES):
                    c, after = cut(t), cut((t + 1) % TILES)
                    p_next, q_next = pond[k + 1, :, after], square[k + 1, :, after]
                    p_right, q_right = pltpu.roll(p, 1, 1), pltpu.roll(q, 1, 1)
                    p_next_left, q_next_left = pltpu.roll(p_next, 127, 1), pltpu.roll(q_next, 127, 1)
                    p_w, p_e = jnp.where(first, p_before, p_right), jnp.where(last, p_next_left, p_left)
                    q_w, q_e = jnp.where(first, q_before, q_right), jnp.where(last, q_next_left, q_left)
                    s = store[k, :, c]
                    soaked = p * pltpu.reciprocal(SCALE + s, approx=True)
                    flow = a_n[k, :, c] * pond[k, :, c] + a_s[k, :, c] * pond[k + 2, :, c]
                    flow = flow + (a_w[k, :, c] * p_w + a_e[k, :, c] * p_e)
                    new_pond[k + 1, :, c] = a_c[k, :, c] * p + flow - soaked
                    inflow = m_n[k, :, c] * square[k, :, c] + m_s[k, :, c] * square[k + 2, :, c]
                    inflow = inflow + (m_w[k, :, c] * q_w + m_e[k, :, c] * q_e)
                    s = (s + soaked) + (inflow - m_c[k, :, c] * q)
                    store[k, :, c] = s
                    new_square[k + 1, :, c] = s * s
                    p, q, p_left, q_left = p_next, q_next, p_next_left, q_next_left
                    p_before, q_before = p_right, q_right
            close(new_pond)
            close(new_square)

        def two(i, carry):
            substep(pond_a, square_a, pond_b, square_b)
            substep(pond_b, square_b, pond_a, square_a)
            return carry

        lax.fori_loop(0, NSUB // 2, two, 0)
        pieces = []
        for last in (pond_a[1 : STRIPS + 1], store[...]):
            pieces.extend(split(last.reshape(STRIPS * 8, WIDE)))
        part = dot(jnp.concatenate(pieces, axis=0), pool_cols[:, 0:128])
        part = jnp.concatenate([part[0:96] + part[96:192], part[192:288] + part[288:384]], axis=1)
        mean = dot(pool_rows[...], both(part)) * (1.0 / (SCALE * AGG * AGG))
        ponded_out[...] = mean[:, 0:128]
        stored_out[...] = mean[:, 128:256]


def moved(array, mesh_shape, target):
    groups, ys, xs = mesh_shape
    pairs = []
    for g in range(groups):
        for y in range(ys):
            for x in range(xs):
                a, b, c = target(g, y, x)
                pairs.append(((g * ys + y) * xs + x, ((a % groups) * ys + b % ys) * xs + c % xs))
    return lax.ppermute(array, ("comp", "gy", "gx"), pairs)


def f32(*shape):
    return jax.ShapeDtypeStruct(shape, F32)


def per_device(
    column_water,
    land_soil,
    level_weight,
    excess_weight,
    soil_weight,
    terrain_class,
    surface_head,
    conductivity,
    active_mask,
    flow_code,
):
    shape = tuple(lax.axis_size(axis) for axis in ("comp", "gy", "gx"))
    group = lax.axis_index("comp")
    params = pltpu.CompilerParams(vmem_limit_bytes=32 * 1024 * 1024)
    arguments = (
        column_water[0].reshape(128, 128), land_soil[0], level_weight[None], excess_weight[None], soil_weight[None],
        terrain_class, surface_head[0], conductivity[0], active_mask[0], flow_code[0],
    )
    hbm = pl.BlockSpec(memory_space=pltpu.HBM)
    fine = f32(ROWS, COLS)
    fine_int = pltpu.VMEM((ROWS, COLS), jnp.int32)
    gxl, gxr, main_up, main_down, gyu, gyd, extra_up, extra_down, water, soil, weight, tabs, terrain, keff, head, code = pl.pallas_call(
        pack_kernel,
        in_specs=[hbm] * 10,
        out_shape=[f32(40, 128)] * 2
        + [f32(56, 128)] * 2
        + [f32(320, 128)] * 2
        + [f32(40, 128)] * 2
        + [f32(128, 128), f32(8, 128), f32(LEV, 128), f32(3, 1, NW)]
        + [jax.ShapeDtypeStruct((ROWS, COLS), jnp.int32)]
        + [fine] * 3,
        scratch_shapes=[
            pltpu.VMEM((128, 128), F32),
            fine_int,
            fine_int,
            pltpu.SemaphoreType.DMA((2 + 5 * CHUNKS,)),
        ],
        compiler_params=params,
        name="pack",
    )(*(pltpu.with_memory_space_constraint(array, pltpu.HBM) for array in arguments))
    ew, sw, up_cols, pool_cols, up_rows, pool_rows = pl.pallas_call(
        ratio_kernel,
        out_shape=[fine] * 2
        + [jax.ShapeDtypeStruct(dims, BF) for dims in ((256, WIDE), (WIDE, 256), (192, 64), (8, 192))],
        scratch_shapes=[pltpu.VMEM((2 * ROWS, COLS), F32)],
        compiler_params=params,
        name="ratio",
    )(tabs, terrain)
    from_left = moved(gxr, shape, lambda g, y, x: (g, y, x + 1))
    from_right = moved(gxl, shape, lambda g, y, x: (g, y, x - 1))
    rows_up = moved(gyd, shape, lambda g, y, x: (g, y + 1, x) if g else (g, y, x ^ 1))
    rows_down = moved(gyu, shape, lambda g, y, x: (g, y - 1, x) if g else (g, y, x ^ 1))
    row = lax.broadcasted_iota(jnp.int32, (8, 128), 0)
    halo = jnp.where(row < 4, from_right[:8], from_left[:8])
    land_up = moved(
        jnp.concatenate([halo, main_down]), shape, lambda g, y, x: (g, y, x ^ 1) if g else (g, y + 1, x)
    )
    land_down = moved(
        jnp.concatenate([halo, main_up]), shape, lambda g, y, x: (g, y, x ^ 1) if g else (g, y - 1, x)
    )
    lane = lax.broadcasted_iota(jnp.int32, (40, 128), 1)
    route_up = moved(
        jnp.concatenate([jnp.where(lane < 100, from_right, from_left), extra_down]), shape, lambda g, y, x: (g, y + 1, x) if g else (g, y, x ^ 1)
    )
    route_down = moved(
        jnp.concatenate([jnp.where(lane < 40, from_right, from_left), extra_up]), shape, lambda g, y, x: (g, y - 1, x) if g else (g, y, x ^ 1)
    )
    coarse, water_top = pl.pallas_call(
        land_kernel,
        out_shape=[f32(2, 16, 256), f32(8, 128)],
        scratch_shapes=[pltpu.VMEM((128, 128), F32), pltpu.VMEM((3, 128, 128), F32)],
        compiler_params=params,
        name="land",
    )(water, soil, weight, from_left, from_right, land_up, land_down)
    arrived = moved(coarse, shape, lambda g, y, x: (1 - g, y, x))
    strips = f32(STRIPS, 8, WIDE)
    ring = pltpu.VMEM((STRIPS + 2, 8, WIDE), F32)
    prepared = pl.pallas_call(
        prepare_kernel,
        out_shape=[strips] * 13,
        scratch_shapes=[
            pltpu.VMEM((128, 128), F32),
            pltpu.VMEM((128, 128), F32),
            pltpu.VMEM((TILES, 96, 128), F32),
            ring,
            ring,
            pltpu.VMEM((32, WIDE), F32),
            pltpu.VMEM((64, WIDE), F32),
            pltpu.VMEM((2 * ROWS, 128), F32),
        ],
        compiler_params=params,
        name="prepare",
    )(
        keff, head, code, ew, sw, tabs, up_cols, pool_cols, from_left, from_right, route_up, route_down,
        rows_up, rows_down, water_top,
    )
    ring = pltpu.VMEM((STRIPS + 2, 8, WIDE), F32)
    ponded, stored = pl.pallas_call(
        route_kernel,
        out_shape=[f32(8, 128), f32(8, 128)],
        scratch_shapes=[ring] * 2 + [pltpu.VMEM((STRIPS, 8, WIDE), F32)] + [ring] * 2,
        compiler_params=params,
        name="route",
    )(arrived, *prepared, up_cols, up_rows, pool_cols, pool_rows)
    returned = moved(stored, shape, lambda g, y, x: (1 - g, y, x))
    land_out = returned / (1.0 + evaporation_scale * water_top * water_top)
    return jnp.where(group == 0, land_out, ponded)[None]


def solution(mesh):
    in_specs = (
        P("comp", None, "gy", "gx"),
        P("comp", "gy", "gx"),
        P(),
        P(),
        P(),
        P("gy", "gx"),
        P("comp", "gy", "gx"),
        P("comp", "gy", "gx"),
        P("comp", "gy", "gx"),
        P("comp", "gy", "gx"),
    )
    out_specs = P("comp", "gy", "gx")
    return jax.shard_map(
        per_device, mesh=mesh, in_specs=in_specs, out_specs=out_specs, check_vma=False
    )
```

```python
import jax
import jax.numpy as jnp
from jax import lax
from jax.experimental import pallas as pl
from jax.experimental.pallas import tpu as pltpu
from jax.sharding import PartitionSpec as P

AGG = 10
NSUB = 8
LEV = 16
ROWS = 80
COLS = 1280
HALO = 8
STRIPS = 12
TILES = 11
WIDE = TILES * 128
CHUNKS = 1
NW = 16
BF = jnp.bfloat16
F32 = jnp.float32

diffusion_rate = 0.2
infiltration_rate = 0.05
drainage_rate = 0.1
half_point = 0.1
evaporation_scale = 0.5
SCALE = 1.0 / infiltration_rate


def split(x):
    high = x.astype(BF)
    return high, (x - high.astype(F32)).astype(BF)


def dot(a, b):
    return jnp.dot(a, b, preferred_element_type=F32)


def both(x):
    return jnp.concatenate(split(x), axis=0)


def inverse(total):
    return float(AGG * AGG) / jnp.where(total > 0.0, total, 1.0)


def twice(x):
    return jnp.concatenate([x, x], axis=1)


def lanes():
    return lax.broadcasted_iota(jnp.int32, (8, 128), 1)


def beside(tiles, lane):
    right = [pltpu.roll(x, 1, 1) for x in tiles]
    left = [pltpu.roll(x, 127, 1) for x in tiles]
    n = len(tiles)
    west = [jnp.where(lane == 0, right[t - 1], right[t]) for t in range(n)]
    east = [jnp.where(lane == 127, left[(t + 1) % n], left[t]) for t in range(n)]
    return west, east


def cut(t):
    return slice(t * 128, (t + 1) * 128)


def within(shape, fine_axis):
    fine = lax.broadcasted_iota(jnp.int32, shape, fine_axis)
    first = AGG * lax.broadcasted_iota(jnp.int32, shape, 1 - fine_axis)
    return jnp.where((fine >= first) & (fine < first + AGG), 1.0, 0.0).astype(BF)


def pack_kernel(
    water_in, soil_in, weight_in, etab_in, stab_in, terrain_in, head_in, cond_in, mask_in, code_in,
    gxl, gxr, main_up, main_down, gyu, gyd, extra_up, extra_down, water, soil, weight, tabs, terrain, keff, head, code,
    square, mask, code_int, sems,
):
    group = lax.axis_index("comp")

    @pl.when(group == 0)
    def _():
        loads = [
            pltpu.make_async_copy(water_in, water, sems.at[0]),
            pltpu.make_async_copy(soil_in, soil, sems.at[1]),
            pltpu.make_async_copy(weight_in, tabs.at[0], sems.at[2]),
        ]
        for load in loads:
            load.start()
        gxl[...] = jnp.zeros((40, 128), F32)
        gxr[...] = jnp.zeros((40, 128), F32)
        square[16:128] = jnp.zeros((112, 128), F32)
        for load in loads:
            load.wait()
        square[0:8] = soil[...]
        square[8:9, 0:LEV] = tabs[0]
        turned = square[...].T
        gxl[3:4] = turned[0:1]
        gxr[4:5] = turned[127:128]
        weight[...] = jnp.broadcast_to(turned[0:LEV, 8:9], (LEV, 128))
        square[...] = water[...].T
        gxl[0:3] = square[0:3]
        gxr[5:8] = square[125:128]
        for j in range(3):
            for h in range(2):
                at = j * 16 + h * 8
                main_up[at : at + 8] = water[pl.ds(h * 64 + j, 8, stride=8), :]
                main_down[at : at + 8] = water[pl.ds(h * 64 + 5 + j, 8, stride=8), :]
        main_up[48:56] = soil[...]
        main_down[48:56] = soil[...]

    @pl.when(group == 1)
    def _():
        load_tabs = [
            pltpu.make_async_copy(etab_in, tabs.at[1], sems.at[0]),
            pltpu.make_async_copy(stab_in, tabs.at[2], sems.at[1]),
        ]
        loads = []
        for i, (source, target) in enumerate(
            ((cond_in, keff), (mask_in, mask), (code_in, code_int), (head_in, head), (terrain_in, terrain))
        ):
            parts = []
            for j in range(CHUNKS):
                rows = pl.ds(j * (ROWS // CHUNKS), ROWS // CHUNKS)
                parts.append(pltpu.make_async_copy(source.at[rows], target.at[rows], sems.at[2 + i * CHUNKS + j]))
                parts[-1].start()
            loads.append(parts)

        for load in load_tabs:
            load.start()

        def ready(i):
            for part in loads[i]:
                part.wait()

        ready(0)
        ready(1)
        keff[...] = keff[...] * mask[...].astype(F32)
        ready(2)
        code[...] = code_int[...].astype(F32)
        ready(3)
        ready(4)

        def terrain_at(r, c):
            return terrain[r, c].astype(F32)

        fields = (lambda r, c: keff[r, c], lambda r, c: head[r, c], lambda r, c: code[r, c], terrain_at)
        for f, field in enumerate(fields):
            for t in range(10):
                at = f * 80 + t * 8
                gyu[at : at + 8] = field(slice(0, 8), cut(t))
                gyd[at : at + 8] = field(slice(ROWS - 8, ROWS), cut(t))
        for t in range(10):
            extra_up[2 * t : 2 * t + 2] = terrain_at(slice(8, 10), cut(t))
            extra_down[2 * t : 2 * t + 2] = terrain_at(slice(ROWS - 10, ROWS - 8), cut(t))
        extra_up[20:40] = jnp.zeros((20, 128), F32)
        extra_down[20:40] = jnp.zeros((20, 128), F32)
        lane = lax.broadcasted_iota(jnp.int32, (ROWS, 128), 1)
        edges = jnp.zeros((ROWS, 128), F32)
        for f, field in enumerate(fields):
            width = 8 if f < 3 else AGG
            first = field(slice(0, ROWS), cut(0))
            last = field(slice(0, ROWS), cut(9))
            first = first if f == 0 else pltpu.roll(first, 8 * f, 1)
            last = pltpu.roll(last, (64 + 8 * f + width) % 128, 1)
            edges = jnp.where((lane >= 8 * f) & (lane < 8 * f + width), first, edges)
            edges = jnp.where((lane >= 64 + 8 * f) & (lane < 64 + 8 * f + width), last, edges)
        square[0:ROWS] = edges
        square[ROWS:128] = jnp.zeros((128 - ROWS, 128), F32)
        square[...] = square[...].T
        gxl[...] = square[0:40]
        gxr[...] = pltpu.roll(square[64:104], 48, 1)
        for load in load_tabs:
            load.wait()


def table_rows(tabs, i):
    return jnp.concatenate([jnp.broadcast_to(tabs[i], (8, NW))] * (128 // NW), axis=1)


def ratio_kernel(tabs, terrain, ew, sw, up_cols, pool_cols, up_rows, pool_rows, found):
    group = lax.axis_index("comp")

    @pl.when(group == 1)
    def _():
        def columns(shape, fine_axis):
            fine = lax.broadcasted_iota(jnp.int32, shape, fine_axis)
            coarse = lax.broadcasted_iota(jnp.int32, shape, 1 - fine_axis)
            first = jnp.where(coarse == 255, WIDE - AGG, jnp.where(coarse <= 128, AGG * coarse, 2 * WIDE))
            return jnp.where((fine >= first) & (fine < first + AGG), 1.0, 0.0).astype(BF)

        up_cols[...] = columns((256, WIDE), 1)
        pool_cols[...] = columns((WIDE, 256), 0)

        def fine_rows(shape, axis):
            at = lax.broadcasted_iota(jnp.int32, shape, axis)
            at = jnp.where(at >= 96, at - 96, at)
            strip = lax.shift_right_logical(at, 3)
            return STRIPS * (at - 8 * strip) + strip

        fine, coarse = fine_rows((192, 64), 0), lax.broadcasted_iota(jnp.int32, (192, 64), 1)
        lower = lax.broadcasted_iota(jnp.int32, (192, 64), 0) >= 96
        mine = jnp.where(coarse >= 32, 1, 0) == jnp.where(lower, 1, 0)
        coarse = lax.rem(coarse, 16)
        own = (fine >= AGG * coarse) & (fine < AGG * coarse + AGG) & (coarse < 8)
        below = (fine >= ROWS) & (fine < ROWS + 8) & (coarse == 8)
        above = (fine >= ROWS + 8) & (coarse == 15)
        up_rows[...] = jnp.where(mine & (own | below | above), 1.0, 0.0).astype(BF)
        fine, coarse = fine_rows((8, 192), 1), lax.broadcasted_iota(jnp.int32, (8, 192), 0)
        pool_rows[...] = jnp.where((fine >= AGG * coarse) & (fine < AGG * coarse + AGG), 1.0, 0.0).astype(BF)

        for i in range(2):
            table = table_rows(tabs, 1 + i)
            for r in range(0, ROWS, 8):
                for t in range(10):
                    found[i * ROWS + r : i * ROWS + r + 8, cut(t)] = jnp.take_along_axis(
                        table, terrain[r : r + 8, cut(t)], axis=1
                    )
        part = dot(both(found[...]), pool_cols[0:COLS, 0:128])
        part = part[0:160] + part[160:320]
        part = jnp.concatenate([part[0:ROWS], part[ROWS:160]], axis=1)
        total = dot(twice(within((8, ROWS), 1)), both(part))
        scale = inverse(total)
        scale = jnp.concatenate([both(scale[:, 0:128]), both(scale[:, 128:256])], axis=0)
        wide = dot(scale, up_cols[0:128, 0:COLS]).astype(BF)
        repeat = twice(within((ROWS, 8), 0))
        ew[...] = found[0:ROWS] * dot(repeat, wide[0:16])
        sw[...] = found[ROWS:160] * dot(repeat, wide[16:32])


def edges_of_grid():
    gy, gx = lax.axis_index("gy"), lax.axis_index("gx")
    has_up = (gy > 0).astype(F32)
    has_down = (gy < lax.axis_size("gy") - 1).astype(F32)
    has_left = (gx > 0).astype(F32)
    has_right = (gx < lax.axis_size("gx") - 1).astype(F32)
    return has_up, has_down, has_left, has_right


def land_kernel(
    water, soil, weight, from_left, from_right, from_up, from_down, coarse, water_out, square, side,
):
    group = lax.axis_index("comp")
    has_up, has_down, has_left, has_right = edges_of_grid()

    @pl.when(group == 0)
    def _():
        pairs = (
            (from_right[0:8], from_left[0:8]),
            (from_down[0:8], from_down[0:8]),
            (from_up[0:8], from_up[0:8]),
        )
        square[8:120] = jnp.zeros((112, 128), F32)
        for i, (right, left) in enumerate(pairs):
            square[0:8] = right
            square[120:128] = left
            side[i] = square[...].T
        lane = lanes()
        for at, (own, down, up) in (
            (0, [pltpu.roll(x[0:8], 5, 0) for x in (from_right, from_down, from_up)]),
            (120, [pltpu.roll(x[0:8], 3, 0) for x in (from_left, from_down, from_up)]),
        ):
            square[at : at + 8] = jnp.where(
                lane < 8, own, jnp.where(lane < 16, pltpu.roll(down, 8, 1), pltpu.roll(up, 16, 1))
            )
        side_soil = square[...].T

        lane2 = lax.broadcasted_iota(jnp.int32, (1, 256), 1)
        col_ok = jnp.where(lane2 < 128, 1.0, jnp.where(lane2 < 192, has_right, has_left))

        def levels(ref, row):
            return jnp.concatenate(
                [ref[pl.ds(h * 64 + row, 8, stride=8), :] for h in range(2)], axis=0
            )

        def side_levels(i, row):
            return jnp.concatenate(
                [side[i, pl.ds(h * 64 + row, 8, stride=8), :] for h in range(2)], axis=0
            )

        field = []
        for j in range(3):
            tile = from_up[8 + j * 16 : 24 + j * 16]
            field.append(jnp.concatenate([tile, side_levels(2, 5 + j)], axis=1) * (col_ok * has_up))
        for j in range(8):
            field.append(jnp.concatenate([levels(water, j), side_levels(0, j)], axis=1) * col_ok)
        for j in range(3):
            tile = from_down[8 + j * 16 : 24 + j * 16]
            field.append(jnp.concatenate([tile, side_levels(1, j)], axis=1) * (col_ok * has_down))

        def sweep(old, first, last):
            new = {}
            for q in range(first, last):
                around = old[q - 1] + old[q + 1] + pltpu.roll(old[q], 1, 1) + pltpu.roll(old[q], 255, 1)
                new[q] = old[q] + diffusion_rate * (around - 4.0 * old[q])
            return new

        once = sweep(field, 1, 13)
        for q in once:
            once[q] = once[q] * (col_ok * (has_up if q < 3 else has_down if q > 10 else 1.0))
        twice = sweep(once, 2, 12)
        for j in range(8):
            water_out[j : j + 1] = twice[3 + j][0:1, 0:128]
        level_weight = jnp.concatenate([weight[...]] * 2, axis=1)
        rain = {q: jnp.sum(level_weight * twice[q] * twice[q], axis=0, keepdims=True) for q in twice}
        blank = jnp.zeros((6, 256), F32)
        rain = jnp.concatenate([rain[3 + j] for j in range(8)] + [rain[11], blank, rain[2]], axis=0)
        moist = jnp.concatenate(
            [
                jnp.concatenate([soil[...], side_soil[0:8]], axis=1),
                jnp.concatenate([from_down[56:57], side_soil[8:9]], axis=1),
                blank,
                jnp.concatenate([from_up[63:64], side_soil[23:24]], axis=1),
            ],
            axis=0,
        )
        coarse[0] = SCALE * rain * moist * moist / (moist * moist + half_point)
        coarse[1] = SCALE * moist


def prepare_kernel(
    keff, head, code, ew, sw, tabs, up_cols, pool_cols, from_left, from_right, from_up, from_down, rows_up, rows_down, after,
    a_e, a_w, a_n, a_s, a_c, m_e, m_w, m_n, m_s, m_c, head_out, ew_out, sw_out,
    square, side, nat, kring, cring, outer, found, near,
):
    group = lax.axis_index("comp")
    has_up, has_down, has_left, has_right = edges_of_grid()

    @pl.when(group == 1)
    def _():
        lane128 = lax.broadcasted_iota(jnp.int32, (40, 128), 1)

        def column(own, down, up):
            return jnp.where(lane128 < 80, own, jnp.where(lane128 < 92, down * has_down, up * has_up))

        square[...] = jnp.zeros((128, 128), F32)
        down, up = from_down[0:40], from_up[0:40]
        square[0:40] = has_right * column(from_right[...], pltpu.roll(down, 80, 1), pltpu.roll(up, 24, 1))
        square[64:104] = has_left * column(
            pltpu.roll(from_left[...], 80, 1), pltpu.roll(down, 32, 1), pltpu.roll(up, 104, 1)
        )
        side[...] = square[...].T
        lane = lax.broadcasted_iota(jnp.int32, (104, 128), 1)

        def columns_of(f, width):
            right = side[0:104] if f == 0 else pltpu.roll(side[0:104], (-8 * f) % 128, 1)
            left = pltpu.roll(side[0:104], (64 - 8 * f - width) % 128, 1)
            return jnp.where(lane < width, right, jnp.where(lane >= 128 - width, left, 0.0))

        def interleave(f):
            for k in range(STRIPS):
                for t in range(TILES):
                    value = nat[t, pl.ds(k, 8, stride=STRIPS), :]
                    if f == 0:
                        kring[k + 1, :, cut(t)] = value
                    elif f == 1:
                        active = kring[k + 1, :, cut(t)] > 0.0
                        head_out[k, :, cut(t)] = jnp.where(active, SCALE * value, 0.0)
                    elif f == 2:
                        cring[k + 1, :, cut(t)] = value
                    elif f == 3:
                        active = kring[k + 1, :, cut(t)] > 0.0
                        ew_out[k, :, cut(t)] = jnp.where(active, value, 0.0)
                    else:
                        sw_out[k, :, cut(t)] = value

        for f, own in enumerate((keff, head, code)):
            for t in range(10):
                at = f * 80 + t * 8
                nat[t, 0:ROWS] = own[:, cut(t)]
                nat[t, ROWS : ROWS + 8] = rows_down[at : at + 8] * has_down
                nat[t, ROWS + 8 : ROWS + 16] = rows_up[at : at + 8] * has_up
            columns = columns_of(f, 8)
            nat[10, 0 : ROWS + 8] = columns[0 : ROWS + 8]
            nat[10, ROWS + 8 : ROWS + 16] = columns[96:104]
            interleave(f)

        corner = columns_of(3, AGG)
        outer[...] = jnp.zeros((32, WIDE), F32)
        for at, rows, extra in ((0, rows_down, from_down), (16, rows_up, from_up)):
            for t in range(10):
                outer[at : at + 8, cut(t)] = rows[240 + t * 8 : 248 + t * 8]
                outer[at + 8 : at + 10, cut(t)] = extra[40 + t * 2 : 42 + t * 2]
        outer[0:10, cut(10)] = corner[80:90]
        outer[16:24, cut(10)] = corner[96:104]
        outer[24:26, cut(10)] = corner[94:96]
        square[0:ROWS] = corner[0:ROWS]
        for i in range(2):
            table = table_rows(tabs, 1 + i)
            for r in range(0, 32, 8):
                for t in range(TILES):
                    found[i * 32 + r : i * 32 + r + 8, cut(t)] = jnp.take_along_axis(
                        table, outer[r : r + 8, cut(t)].astype(jnp.int32), axis=1
                    )
            for r in range(0, ROWS, 8):
                near[i * ROWS + r : i * ROWS + r + 8] = jnp.take_along_axis(
                    table, square[r : r + 8].astype(jnp.int32), axis=1
                )
        part = dot(both(found[...]), pool_cols[...])
        part = part[0:64] + part[64:128]
        totals = []
        for at in (0, 16, 32, 48):
            totals.append(jnp.sum(part[at : at + 8], axis=0, keepdims=True) + part[at + 8 : at + 9] + part[at + 9 : at + 10])
        scale = inverse(jnp.concatenate(totals + [jnp.zeros((4, 256), F32)], axis=0))
        wide = dot(both(scale), up_cols[...])
        wide = wide[0:8] + wide[8:16]

        col = lax.broadcasted_iota(jnp.int32, (128, 128), 1)
        row = lax.broadcasted_iota(jnp.int32, (128, 128), 0)
        ends = jnp.where(((col == 0) & (row < AGG)) | ((col == 1) & (row >= 128 - AGG)), 1.0, 0.0).astype(BF)
        part = dot(both(near[...]), ends)
        part = part[0:160] + part[160:320]
        part = jnp.concatenate([part[0:ROWS], part[ROWS:160]], axis=1)
        scale = inverse(dot(twice(within((8, ROWS), 1)), both(part)))
        scale = dot(twice(within((ROWS, 8), 0)), both(scale))
        first = lax.broadcasted_iota(jnp.int32, (ROWS, 128), 1) < AGG
        for i, own in enumerate((ew, sw)):
            for t in range(TILES):
                nat[t, ROWS : ROWS + 8] = found[32 * i : 32 * i + 8, cut(t)] * wide[2 * i : 2 * i + 1, cut(t)]
                nat[t, ROWS + 8 : ROWS + 16] = (
                    found[32 * i + 16 : 32 * i + 24, cut(t)] * wide[2 * i + 1 : 2 * i + 2, cut(t)]
                )
            at = 128 * i
            nat[10, 0:ROWS] = near[i * ROWS : (i + 1) * ROWS] * jnp.where(
                first, scale[:, at : at + 1], scale[:, at + 1 : at + 2]
            )
            for t in range(10):
                nat[t, 0:ROWS] = own[:, cut(t)]
            interleave(3 + i)
        for ring in (kring, cring):
            for t in range(TILES):
                ring[0, :, cut(t)] = pltpu.roll(ring[STRIPS, :, cut(t)], 1, 0)
                ring[STRIPS + 1, :, cut(t)] = pltpu.roll(ring[1, :, cut(t)], 7, 0)

        lane = lanes()
        for k in range(STRIPS):
            here = [kring[k + 1, :, cut(t)] for t in range(TILES)]
            codes = [cring[k + 1, :, cut(t)] for t in range(TILES)]
            west, east = beside(here, lane)

            def drains(cond, codes, number):
                return jnp.where((cond > 0.0) & (codes == number), drainage_rate / SCALE, 0.0)

            to_east, _ = beside([drains(here[t], codes[t], 3.0) for t in range(TILES)], lane)
            _, to_west = beside([drains(here[t], codes[t], 2.0) for t in range(TILES)], lane)
            for t in range(TILES):
                north, south = kring[k, :, cut(t)], kring[k + 2, :, cut(t)]
                n, s = jnp.sqrt(here[t] * north), jnp.sqrt(here[t] * south)
                w, e = jnp.sqrt(here[t] * west[t]), jnp.sqrt(here[t] * east[t])
                a_n[k, :, cut(t)] = n
                a_s[k, :, cut(t)] = s
                a_w[k, :, cut(t)] = w
                a_e[k, :, cut(t)] = e
                a_c[k, :, cut(t)] = 1.0 - ((n + s) + (w + e))
                m_n[k, :, cut(t)] = drains(north, cring[k, :, cut(t)], 1.0)
                m_s[k, :, cut(t)] = drains(south, cring[k + 2, :, cut(t)], 0.0)
                m_w[k, :, cut(t)] = to_east[t]
                m_e[k, :, cut(t)] = to_west[t]
                m_c[k, :, cut(t)] = jnp.where(here[t] > 0.0, drainage_rate / SCALE, 0.0)


def route_kernel(
    coarse, a_e, a_w, a_n, a_s, a_c, m_e, m_w, m_n, m_s, m_c, head, ew, sw, up_cols, up_rows, pool_cols, pool_rows,
    ponded_out, stored_out, pond_a, pond_b, store, square_a, square_b,
):
    group = lax.axis_index("comp")

    @pl.when(group == 1)
    def _():
        pieces = jnp.concatenate([*split(coarse[0]), *split(coarse[1])], axis=0)
        fields = dot(up_rows[...], dot(pieces, up_cols[...]).astype(BF))
        excess, moist = fields[0:96], fields[96:192]
        pond_a[1 : STRIPS + 1] = head[...] + ew[...] * excess.reshape(STRIPS, 8, WIDE)
        store[...] = sw[...] * moist.reshape(STRIPS, 8, WIDE)
        square_a[1 : STRIPS + 1] = store[...] * store[...]

        def close(ring):
            for t in range(TILES):
                ring[0, :, cut(t)] = pltpu.roll(ring[STRIPS, :, cut(t)], 1, 0)
                ring[STRIPS + 1, :, cut(t)] = pltpu.roll(ring[1, :, cut(t)], 7, 0)

        close(pond_a)
        close(square_a)

        def substep(pond, square, new_pond, new_square):
            lane = lanes()
            first, last = lane == 0, lane == 127
            for k in range(STRIPS):
                p, q = pond[k + 1, :, cut(0)], square[k + 1, :, cut(0)]
                p_left, q_left = pltpu.roll(p, 127, 1), pltpu.roll(q, 127, 1)
                p_before = pltpu.roll(pond[k + 1, :, cut(TILES - 1)], 1, 1)
                q_before = pltpu.roll(square[k + 1, :, cut(TILES - 1)], 1, 1)
                for t in range(TILES):
                    c, after = cut(t), cut((t + 1) % TILES)
                    p_next, q_next = pond[k + 1, :, after], square[k + 1, :, after]
                    p_right, q_right = pltpu.roll(p, 1, 1), pltpu.roll(q, 1, 1)
                    p_next_left, q_next_left = pltpu.roll(p_next, 127, 1), pltpu.roll(q_next, 127, 1)
                    p_w, p_e = jnp.where(first, p_before, p_right), jnp.where(last, p_next_left, p_left)
                    q_w, q_e = jnp.where(first, q_before, q_right), jnp.where(last, q_next_left, q_left)
                    s = store[k, :, c]
                    soaked = p * pltpu.reciprocal(SCALE + s, approx=True)
                    flow = a_n[k, :, c] * pond[k, :, c] + a_s[k, :, c] * pond[k + 2, :, c]
                    flow = flow + (a_w[k, :, c] * p_w + a_e[k, :, c] * p_e)
                    new_pond[k + 1, :, c] = a_c[k, :, c] * p + flow - soaked
                    inflow = m_n[k, :, c] * square[k, :, c] + m_s[k, :, c] * square[k + 2, :, c]
                    inflow = inflow + (m_w[k, :, c] * q_w + m_e[k, :, c] * q_e)
                    s = (s + soaked) + (inflow - m_c[k, :, c] * q)
                    store[k, :, c] = s
                    new_square[k + 1, :, c] = s * s
                    p, q, p_left, q_left = p_next, q_next, p_next_left, q_next_left
                    p_before, q_before = p_right, q_right
            close(new_pond)
            close(new_square)

        def two(i, carry):
            substep(pond_a, square_a, pond_b, square_b)
            substep(pond_b, square_b, pond_a, square_a)
            return carry

        lax.fori_loop(0, NSUB // 2, two, 0)
        pieces = []
        for last in (pond_a[1 : STRIPS + 1], store[...]):
            pieces.extend(split(last.reshape(STRIPS * 8, WIDE)))
        part = dot(jnp.concatenate(pieces, axis=0), pool_cols[:, 0:128])
        part = jnp.concatenate([part[0:96] + part[96:192], part[192:288] + part[288:384]], axis=1)
        mean = dot(pool_rows[...], both(part)) * (1.0 / (SCALE * AGG * AGG))
        ponded_out[...] = mean[:, 0:128]
        stored_out[...] = mean[:, 128:256]


def moved(array, mesh_shape, target):
    groups, ys, xs = mesh_shape
    pairs = []
    for g in range(groups):
        for y in range(ys):
            for x in range(xs):
                a, b, c = target(g, y, x)
                pairs.append(((g * ys + y) * xs + x, ((a % groups) * ys + b % ys) * xs + c % xs))
    return lax.ppermute(array, ("comp", "gy", "gx"), pairs)


def f32(*shape):
    return jax.ShapeDtypeStruct(shape, F32)


def per_device(
    column_water,
    land_soil,
    level_weight,
    excess_weight,
    soil_weight,
    terrain_class,
    surface_head,
    conductivity,
    active_mask,
    flow_code,
):
    shape = tuple(lax.axis_size(axis) for axis in ("comp", "gy", "gx"))
    group = lax.axis_index("comp")
    params = pltpu.CompilerParams(vmem_limit_bytes=32 * 1024 * 1024)
    arguments = (
        column_water[0].reshape(128, 128), land_soil[0], level_weight[None], excess_weight[None], soil_weight[None],
        terrain_class, surface_head[0], conductivity[0], active_mask[0], flow_code[0],
    )
    hbm = pl.BlockSpec(memory_space=pltpu.HBM)
    fine = f32(ROWS, COLS)
    fine_int = pltpu.VMEM((ROWS, COLS), jnp.int32)
    gxl, gxr, main_up, main_down, gyu, gyd, extra_up, extra_down, water, soil, weight, tabs, terrain, keff, head, code = pl.pallas_call(
        pack_kernel,
        in_specs=[hbm] * 10,
        out_shape=[f32(40, 128)] * 2
        + [f32(56, 128)] * 2
        + [f32(320, 128)] * 2
        + [f32(40, 128)] * 2
        + [f32(128, 128), f32(8, 128), f32(LEV, 128), f32(3, 1, NW)]
        + [jax.ShapeDtypeStruct((ROWS, COLS), jnp.int32)]
        + [fine] * 3,
        scratch_shapes=[
            pltpu.VMEM((128, 128), F32),
            fine_int,
            fine_int,
            pltpu.SemaphoreType.DMA((2 + 5 * CHUNKS,)),
        ],
        compiler_params=params,
        name="pack",
    )(*(pltpu.with_memory_space_constraint(array, pltpu.HBM) for array in arguments))
    ew, sw, up_cols, pool_cols, up_rows, pool_rows = pl.pallas_call(
        ratio_kernel,
        out_shape=[fine] * 2
        + [jax.ShapeDtypeStruct(dims, BF) for dims in ((256, WIDE), (WIDE, 256), (192, 64), (8, 192))],
        scratch_shapes=[pltpu.VMEM((2 * ROWS, COLS), F32)],
        compiler_params=params,
        name="ratio",
    )(tabs, terrain)
    from_left = moved(gxr, shape, lambda g, y, x: (g, y, x + 1))
    from_right = moved(gxl, shape, lambda g, y, x: (g, y, x - 1))
    rows_up = moved(gyd, shape, lambda g, y, x: (g, y + 1, x) if g else (g, y, x ^ 1))
    rows_down = moved(gyu, shape, lambda g, y, x: (g, y - 1, x) if g else (g, y, x ^ 1))
    row = lax.broadcasted_iota(jnp.int32, (8, 128), 0)
    halo = jnp.where(row < 4, from_right[:8], from_left[:8])
    land_up = moved(
        jnp.concatenate([halo, main_down]), shape, lambda g, y, x: (g, y, x ^ 1) if g else (g, y + 1, x)
    )
    land_down = moved(
        jnp.concatenate([halo, main_up]), shape, lambda g, y, x: (g, y, x ^ 1) if g else (g, y - 1, x)
    )
    lane = lax.broadcasted_iota(jnp.int32, (40, 128), 1)
    route_up = moved(
        jnp.concatenate([jnp.where(lane < 100, from_right, from_left), extra_down]), shape, lambda g, y, x: (g, y + 1, x) if g else (g, y, x ^ 1)
    )
    route_down = moved(
        jnp.concatenate([jnp.where(lane < 40, from_right, from_left), extra_up]), shape, lambda g, y, x: (g, y - 1, x) if g else (g, y, x ^ 1)
    )
    coarse, water_top = pl.pallas_call(
        land_kernel,
        out_shape=[f32(2, 16, 256), f32(8, 128)],
        scratch_shapes=[pltpu.VMEM((128, 128), F32), pltpu.VMEM((3, 128, 128), F32)],
        compiler_params=params,
        name="land",
    )(water, soil, weight, from_left, from_right, land_up, land_down)
    arrived = moved(coarse, shape, lambda g, y, x: (1 - g, y, x))
    strips = f32(STRIPS, 8, WIDE)
    ring = pltpu.VMEM((STRIPS + 2, 8, WIDE), F32)
    prepared = pl.pallas_call(
        prepare_kernel,
        out_shape=[strips] * 13,
        scratch_shapes=[
            pltpu.VMEM((128, 128), F32),
            pltpu.VMEM((128, 128), F32),
            pltpu.VMEM((TILES, 96, 128), F32),
            ring,
            ring,
            pltpu.VMEM((32, WIDE), F32),
            pltpu.VMEM((64, WIDE), F32),
            pltpu.VMEM((2 * ROWS, 128), F32),
        ],
        compiler_params=params,
        name="prepare",
    )(
        keff, head, code, ew, sw, tabs, up_cols, pool_cols, from_left, from_right, route_up, route_down,
        rows_up, rows_down, water_top,
    )
    ring = pltpu.VMEM((STRIPS + 2, 8, WIDE), F32)
    ponded, stored = pl.pallas_call(
        route_kernel,
        out_shape=[f32(8, 128), f32(8, 128)],
        scratch_shapes=[ring] * 2 + [pltpu.VMEM((STRIPS, 8, WIDE), F32)] + [ring] * 2,
        compiler_params=params,
        name="route",
    )(arrived, *prepared, up_cols, up_rows, pool_cols, pool_rows)
    returned = moved(stored, shape, lambda g, y, x: (1 - g, y, x))
    land_out = returned / (1.0 + evaporation_scale * water_top * water_top)
    return jnp.where(group == 0, land_out, ponded)[None]


def solution(mesh):
    in_specs = (
        P("comp", None, "gy", "gx"),
        P("comp", "gy", "gx"),
        P(),
        P(),
        P(),
        P("gy", "gx"),
        P("comp", "gy", "gx"),
        P("comp", "gy", "gx"),
        P("comp", "gy", "gx"),
        P("comp", "gy", "gx"),
    )
    out_specs = P("comp", "gy", "gx")
    return jax.shard_map(
        per_device, mesh=mesh, in_specs=in_specs, out_specs=out_specs, check_vma=False
    )
```
